256 devices in a mesh: chan: 32 (over z, y_hi, core), tile: 8 (over x, y_lo).
Axes of the slice: x: 4, y: 4 (y_hi: 2, y_lo: 2; y = y_hi * 2 + y_lo), z: 8, core: 2. Of those that a mesh axis runs over, the one named last changes fastest.
Arguments:
- voltages: int32 [2, 512, 323584], P(None, ('tile', 'chan')), may hold values from -128 to 127
- filter_taps: float32 [16, 4096], replicated, may hold values from -0.02 to 0.02
Outputs:
- visibilities: bfloat16 [2048, 512, 512], P(('chan', 'tile'))
The draws below stay inside these ranges and needn't reach their ends.
All inputs are finite; a program needn't handle non-finite values.
Results may differ from the reference program's by a relative error of at most 0.0055.
Values may be sent and summed in bfloat16 or wider, within the bound.
A program may use at most 64 MiB of HBM per device.

```python
import math
import jax
import jax.numpy as jnp
from jax import lax

INPUTS = 512
NFFT = 4096
TAPS = 16
SPEC = 64
KEEP = 2048


def set_ends(result, own_key, low, top_value):
    longest = result.shape.index(max(result.shape))
    spots = []
    for shift in (0, 1):
        where = [jax.random.randint(jax.random.fold_in(own_key, axis), (), 0, length) for axis, length in enumerate(result.shape)]
        where[longest] = (where[longest] + shift) % result.shape[longest]
        spots.append(tuple(where))
    return result.at[spots[0]].set(low).at[spots[1]].set(top_value)


def noise(own_key, dims, deviation, reach, kind=jnp.bfloat16):
    result = deviation * jax.random.normal(own_key, dims, jnp.float32)
    return jnp.clip(result, min=-reach, max=reach).astype(kind)


def setup_inputs(seed: int = 0) -> dict:
    streams_of = jax.random.split(jax.random.key(seed), 3)
    voltages = set_ends(jax.random.randint(streams_of[0], (2, INPUTS, (SPEC + TAPS - 1) * NFFT), -128, 128), jax.random.fold_in(streams_of[0], 1), -128, 127).astype(jnp.int32)
    filter_taps = noise(streams_of[1], (TAPS, NFFT), 0.0034, 0.02, jnp.float32)
    return {"voltages": voltages, "filter_taps": filter_taps}


def channelize_one(signal, filter_taps):
    samples = signal.astype(jnp.float32).reshape(2, SPEC + TAPS - 1, NFFT)
    filtered = filter_taps[0] * samples[:, 0:SPEC]
    for tap_index in range(1, TAPS):
        filtered = filtered + filter_taps[tap_index] * samples[:, tap_index:tap_index + SPEC]
    spectrum = jnp.fft.fft(lax.complex(filtered[0], filtered[1]), axis=-1)[:, :KEEP]
    spectrum = spectrum * (1.0 / math.sqrt(NFFT))
    return jnp.concatenate([jnp.real(spectrum).T, jnp.imag(spectrum).T], axis=1).astype(jnp.bfloat16)

def correlate_one(channel_data):
    real_part = channel_data[:, :SPEC]
    imag_part = channel_data[:, SPEC:]
    swapped = jnp.concatenate([imag_part, -real_part], axis=1)
    stacked = jnp.concatenate([channel_data, swapped], axis=0)
    product = jnp.dot(stacked, channel_data.T, preferred_element_type=jnp.float32)
    row_index = jnp.arange(INPUTS, dtype=jnp.int32)[:, None]
    col_index = jnp.arange(INPUTS, dtype=jnp.int32)[None, :]
    packed = jnp.where(row_index <= col_index, product[:INPUTS], product[INPUTS:])
    return (packed * (1.0 / SPEC)).astype(jnp.bfloat16)

def reference(voltages, filter_taps):
    per_signal = jnp.transpose(voltages, (1, 0, 2))
    spectra = lax.map(lambda signal: channelize_one(signal, filter_taps), per_signal)
    spectra = jnp.transpose(spectra, (1, 0, 2))
    return lax.map(correlate_one, spectra)
```

```python
import functools
import math

import jax
import jax.numpy as jnp
import ml_dtypes
import numpy as np
from jax import lax
from jax.experimental import pallas as pl
from jax.experimental.pallas import tpu as pltpu
from jax.sharding import PartitionSpec as P

MESH = pl.DeviceIdType.MESH
NFFT, TAPS, SPEC, KEEP = 4096, 16, 64, 2048
FRAMES = SPEC + TAPS - 1
LANES = 128
R1 = NFFT // LANES
C2 = KEEP // R1
SB = 8
CHUNKS = -(-FRAMES // SB)
NT = (((1,), (1,)), ((), ()))


def split(values):
    high = values.astype(ml_dtypes.bfloat16)
    low = (values - high.astype(np.float64)).astype(ml_dtypes.bfloat16)
    return high, low


@functools.cache
def first_table():
    c1, j = np.meshgrid(np.arange(R1), np.arange(R1), indexing="ij")
    angle = 2 * math.pi * ((c1 * j) % R1) / R1
    cos, sin = np.cos(angle), np.sin(angle)
    unit = np.stack([np.stack([cos, sin], 1), np.stack([-sin, cos], 1)], 0)
    eye = np.eye(2)
    full = np.einsum("ab,rcpj,st->asrcbpjt", eye, unit, eye).reshape(256, 256)
    return np.concatenate(split(full), 0)


@functools.cache
def second_table():
    chan = np.arange(R1)[:, None, None] + R1 * np.arange(C2)[None, :, None]
    angle = 2 * math.pi * ((chan * np.arange(LANES)) % NFFT) / NFFT
    full = np.concatenate([np.cos(angle), -np.sin(angle)], 2) / math.sqrt(NFFT)
    return np.concatenate(split(full), 1)


def place():
    chan, tile = lax.axis_index("chan"), lax.axis_index("tile")
    return chan // 4, (chan // 2) % 2, chan % 2, tile


def z_shift(step):
    back = 7 - step
    return jnp.where(back % 2 == 1, (back + 1) // 2, (8 - back // 2) % 8)


def chan_peer(step):
    z, high, core, tile = place()
    step = 32 - step
    z = (z + z_shift(7 - step % 8)) % 8
    return {"chan": z * 4 + ((high + (step // 8) % 2) % 2) * 2 + (core + step // 16) % 2, "tile": tile}


def tile_peer(step):
    return {"chan": lax.axis_index("chan"), "tile": (lax.axis_index("tile") + step) % 8}


def signal_all(sem, peer, count):
    def body(step, carry):
        pl.semaphore_signal(sem, inc=1, device_id=peer(step), device_id_type=MESH)
        return carry

    lax.fori_loop(1, count, body, 0)


def channelize(v_hbm, h_hbm, d_hbm, w_hbm, got, vbuf, hraw, hbuf, dbuf, wbuf, xs, af, sbuf, msg, vsem, csem, send, recv, ready):
    barrier = pltpu.get_barrier_semaphore()
    chan, tile = lax.axis_index("chan"), lax.axis_index("tile")
    me = tile * 32 + chan

    taps_in = pltpu.make_async_copy(h_hbm, hraw, csem.at[0])
    taps_in.start()
    frames_in = []
    for chunk in range(CHUNKS):
        count = min(SB, FRAMES - chunk * SB)
        where = pl.ds(chunk * SB, count)
        frames_in.append(pltpu.make_async_copy(v_hbm.at[:, where], vbuf.at[:, where], vsem.at[chunk]))
    for chunk in range(3):
        frames_in[chunk].start()
    first_in = pltpu.make_async_copy(d_hbm, dbuf, csem.at[1])
    first_in.start()
    for chunk in range(3, CHUNKS):
        frames_in[chunk].start()
    second_in = pltpu.make_async_copy(w_hbm, wbuf, csem.at[2])
    second_in.start()

    signal_all(barrier, chan_peer, 32)
    signal_all(barrier, tile_peer, 8)

    taps_in.wait()
    for j in range(R1):
        row = hraw[:, j * LANES : (j + 1) * LANES]
        hbuf[:, 2 * j : 2 * j + 2, :] = jnp.broadcast_to(row[:, None, :], (TAPS, 2, LANES))
    frames_in[0].wait()
    frames_in[1].wait()
    frames_in[2].wait()
    first_in.wait()

    def filter_rows(part, row, base):
        rows = pl.ds(row, 8)
        window = vbuf[part, pl.ds(base, SB + TAPS - 1), rows, :].astype(jnp.float32)
        total = hbuf[0, rows, :][None] * window[0:SB]
        for tap in range(1, TAPS):
            total = total + hbuf[tap, rows, :][None] * window[tap : tap + SB]
        return total

    def filter_block(block):
        base = block * SB
        for part in range(2):
            for pair in range(4):
                row = pair * 16
                both = jnp.concatenate([filter_rows(part, row, base), filter_rows(part, row + 8, base)], axis=1)
                xs[:, part * 64 + row : part * 64 + row + 16, :] = both.astype(jnp.bfloat16)
        for half in range(SB // 4):
            right = jnp.concatenate(
                [xs[half * 4 + 2 * q : half * 4 + 2 * q + 2].reshape(256, LANES) for q in range(2)], axis=1
            )
            out = jnp.dot(dbuf[...], right, preferred_element_type=jnp.float32)
            out = out[:256] + out[256:]
            for q in range(2):
                af[pl.ds(pl.multiple_of((base + half * 4 + 2 * q) * 128, 256), 256), :] = out[:, q * 128 : (q + 1) * 128]

    for block in range(SPEC // SB):
        if block:
            frames_in[block + 2].wait()
        filter_block(block)

    pl.semaphore_wait(barrier, 38)
    signal_all(ready, tile_peer, 8)
    second_in.wait()

    def group_step(turn, carry):
        group = (tile + turn) % 4
        for k in range(8):
            c1 = group * 8 + k
            rows = []
            for sig in range(2):
                real = af[pl.ds(sig * 64 + c1, SPEC, stride=128), :]
                imag = af[pl.ds(sig * 64 + R1 + c1, SPEC, stride=128), :]
                rows.append(jnp.concatenate([real, -imag], axis=1))
                rows.append(jnp.concatenate([imag, real], axis=1))
            right = jnp.concatenate(rows, axis=0).astype(jnp.bfloat16)
            out = lax.dot_general(wbuf[c1], right, NT, preferred_element_type=jnp.float32)
            out = out[:C2] + out[C2:]
            for sig in range(2):
                sbuf[(2 * k + sig) * C2 : (2 * k + sig + 1) * C2, :] = out[:, sig * 128 : (sig + 1) * 128]
        for c2 in range(C2):
            msg[turn * C2 + c2] = sbuf[pl.ds(c2, 16, stride=C2), :].astype(jnp.bfloat16)

        @pl.when(turn == 0)
        def _():
            pl.semaphore_wait(ready, 7)

        z, high, core, _ = place()

        def send_step(step, carry):
            to_core = (core + step % 2) % 2
            to_z = (z + z_shift(step // 2 % 8)) % 8
            to_high = (high + step // 16 % 2) % 2
            half = (tile // 4 + step // 32) % 2
            to_chan = to_z * 4 + to_high * 2 + to_core
            to_tile = half * 4 + group

            @pl.when(jnp.logical_or(to_chan != chan, to_tile != tile))
            def _():
                pltpu.make_async_remote_copy(
                    src_ref=msg.at[turn * C2 + 2 * to_chan + half],
                    dst_ref=got.at[me],
                    send_sem=send,
                    recv_sem=recv,
                    device_id={"chan": to_chan, "tile": to_tile},
                    device_id_type=MESH,
                ).start()

            return carry

        lax.fori_loop(0, C2, send_step, 0)
        return carry

    lax.fori_loop(0, 4, group_step, 0)
    got[me] = msg[2 * chan + tile // 4]
    all_but_one = pl.ds(0, 255)
    pltpu.make_async_copy(msg.at[all_but_one], got.at[all_but_one], send).wait()
    pltpu.make_async_copy(msg.at[all_but_one], got.at[all_but_one], recv).wait()


def correlate(got, out, ordered, swapped):
    k = pl.program_id(0)

    @pl.when(k == 0)
    def _():
        to = lax.broadcasted_iota(jnp.int32, (256, 256), 0)
        come = lax.broadcasted_iota(jnp.int32, (256, 256), 1)
        sort = (to == (come // 2 % 8) * 32 + (come // 16) * 2 + come % 2).astype(jnp.bfloat16)
        for block in range(8):
            right = jnp.concatenate(
                [got[(2 * block + q) * 16 : (2 * block + q + 1) * 16].reshape(256, LANES) for q in range(2)], axis=1
            )
            rows = jnp.dot(sort, right, preferred_element_type=jnp.float32)
            for q in range(2):
                part = rows[:, q * 128 : (q + 1) * 128]
                turned = jnp.concatenate([part[:, SPEC:], -part[:, :SPEC]], axis=1)
                here = pl.ds((2 * block + q) * 32, 32)
                ordered[:, here, :] = part.reshape(8, 32, LANES).astype(jnp.bfloat16)
                swapped[:, here, :] = turned.reshape(8, 32, LANES).astype(jnp.bfloat16)

    def product(left, lo, right, hi):
        return lax.dot_general(
            left[k, lo * 256 : lo * 256 + 256, :],
            right[k, hi * 256 : hi * 256 + 256, :],
            NT,
            preferred_element_type=jnp.float32,
        )

    upper = lax.broadcasted_iota(jnp.int32, (256, 256), 0) <= lax.broadcasted_iota(jnp.int32, (256, 256), 1)
    for lo in range(2):
        for hi in range(2):
            if lo < hi:
                block = product(ordered, lo, ordered, hi)
            elif lo > hi:
                block = product(swapped, lo, ordered, hi)
            else:
                block = jnp.where(upper, product(ordered, lo, ordered, hi), product(swapped, lo, ordered, hi))
            out[0, lo * 256 : lo * 256 + 256, hi * 256 : hi * 256 + 256] = (block * (1.0 / SPEC)).astype(jnp.bfloat16)


def per_device(voltages, filter_taps):
    rows = NFFT // LANES
    frames = voltages.reshape(2, 2, FRAMES * rows, LANES).transpose(0, 2, 1, 3).reshape(2, FRAMES, 2 * rows, LANES)
    first, second = first_table(), second_table()
    vmem, anywhere = pl.BlockSpec(memory_space=pltpu.VMEM), pl.BlockSpec(memory_space=pl.ANY)
    dma = pltpu.SemaphoreType.DMA
    got = pl.pallas_call(
        channelize,
        name="channelize",
        out_shape=jax.ShapeDtypeStruct((256, 16, LANES), jnp.bfloat16),
        in_specs=[anywhere] * 4,
        out_specs=vmem,
        scratch_shapes=[
            pltpu.VMEM((2, FRAMES, 2 * rows, LANES), jnp.int32),
            pltpu.VMEM((TAPS, NFFT), jnp.float32),
            pltpu.VMEM((TAPS, 2 * rows, LANES), jnp.float32),
            pltpu.VMEM(first.shape, jnp.bfloat16),
            pltpu.VMEM(second.shape, jnp.bfloat16),
            pltpu.VMEM((SB, 4 * rows, LANES), jnp.bfloat16),
            pltpu.VMEM((SPEC * 128, LANES), jnp.float32),
            pltpu.VMEM((16 * C2, LANES), jnp.float32),
            pltpu.VMEM((256, 16, LANES), jnp.bfloat16),
            dma((CHUNKS,)),
            dma((3,)),
            dma,
            dma,
            pltpu.SemaphoreType.REGULAR,
        ],
        compiler_params=pltpu.CompilerParams(collective_id=0, has_side_effects=True, vmem_limit_bytes=60 << 20),
    )(frames, filter_taps, jnp.asarray(first), jnp.asarray(second))
    return pl.pallas_call(
        correlate,
        name="correlate",
        out_shape=jax.ShapeDtypeStruct((8, 512, 512), jnp.bfloat16),
        grid=(8,),
        in_specs=[pl.BlockSpec((256, 16, LANES), lambda k: (0, 0, 0))],
        out_specs=pl.BlockSpec((1, 512, 512), lambda k: (k, 0, 0)),
        scratch_shapes=[pltpu.VMEM((8, 512, LANES), jnp.bfloat16)] * 2,
        compiler_params=pltpu.CompilerParams(vmem_limit_bytes=32 << 20),
    )(got)


def solution(mesh):
    return jax.shard_map(
        per_device,
        mesh=mesh,
        in_specs=(P(None, ("tile", "chan"), None), P()),
        out_specs=P(("chan", "tile"), None, None),
        check_vma=False,
    )
```

```python
import functools
import math

import jax
import jax.numpy as jnp
import ml_dtypes
import numpy as np
from jax import lax
from jax.experimental import pallas as pl
from jax.experimental.pallas import tpu as pltpu
from jax.sharding import PartitionSpec as P

MESH = pl.DeviceIdType.MESH
NFFT, TAPS, SPEC, KEEP = 4096, 16, 64, 2048
FRAMES = SPEC + TAPS - 1
LANES = 128
R1 = NFFT // LANES
C2 = KEEP // R1
SB = 16
BLOCKS = SPEC // SB
FIRST = SB + TAPS - 1
HALF = TAPS // 2
NT = (((1,), (1,)), ((), ()))


def split(values):
    high = values.astype(ml_dtypes.bfloat16)
    low = (values - high.astype(np.float64)).astype(ml_dtypes.bfloat16)
    return high, low


@functools.cache
def first_table():
    c1, j = np.meshgrid(np.arange(R1), np.arange(R1), indexing="ij")
    angle = 2 * math.pi * ((c1 * j) % R1) / R1
    cos, sin = np.cos(angle), np.sin(angle)
    unit = np.concatenate([np.concatenate([cos, sin], 1), np.concatenate([-sin, cos], 1)], 0)
    return np.concatenate(split(np.kron(np.eye(4), unit)), 0)


@functools.cache
def second_table():
    chan = np.arange(R1)[:, None, None] + R1 * np.arange(C2)[None, :, None]
    angle = 2 * math.pi * ((chan * np.arange(LANES)) % NFFT) / NFFT
    full = np.concatenate([np.cos(angle), -np.sin(angle)], 2) / math.sqrt(NFFT)
    return np.concatenate(split(full), 1)


Z_ORDER = (4, 3, 5, 2, 6, 1, 7, 0)


def chan_table():
    chan = lax.axis_index("chan")
    z, high, core = lax.div(chan, 4), lax.rem(lax.div(chan, 2), 2), lax.rem(chan, 2)
    z_part = [lax.rem(z + dz, 8) * 4 for dz in range(8)]
    y_part = [high * 2, 2 - high * 2]
    c_part = [core, 1 - core]
    return chan, {(dz, dh, dc): z_part[dz] + (y_part[dh] + c_part[dc]) for dz in range(8) for dh in range(2) for dc in range(2)}


def signal(sem, chan, tile):
    pl.semaphore_signal(sem, inc=1, device_id={"chan": chan, "tile": tile}, device_id_type=MESH)


def channelize(v_hbm, h_hbm, d_hbm, w_hbm, out_hbm, vbuf, hraw, hbuf, dbuf, wbuf, xs, af, sbuf, msg, got, ordered, vsem, csem, osem, send, recv, ready):
    barrier = pltpu.get_barrier_semaphore()
    chan, chan_at = chan_table()
    tile = lax.axis_index("tile")
    tile_at = [lax.rem(tile + step, 8) for step in range(8)]
    me = tile * 32 + chan

    def frames_in(part, chunk):
        where = pl.ds(0, FIRST) if isinstance(chunk, int) and chunk == 0 else pl.ds(chunk * SB + TAPS - 1, SB)
        return pltpu.make_async_copy(v_hbm.at[part, where], vbuf.at[part, where], vsem.at[part, chunk])

    taps_in = pltpu.make_async_copy(h_hbm, hraw, csem.at[0])
    first_in = pltpu.make_async_copy(d_hbm, dbuf, csem.at[1])
    second_in = pltpu.make_async_copy(w_hbm, wbuf, csem.at[2])
    taps_in.start()
    frames_in(0, 0).start()
    frames_in(1, 0).start()
    first_in.start()
    for chunk in range(1, BLOCKS):
        for part in range(2):
            frames_in(part, chunk).start()
    second_in.start()

    for dz in Z_ORDER:
        for dh in range(2):
            for dc in range(2):
                if dz or dh or dc:
                    signal(barrier, chan_at[dz, dh, dc], tile)
    for step in range(1, 8):
        signal(barrier, chan, tile_at[step])

    taps_in.wait()
    for block in range(4):
        for i in range(HALF):
            even, odd = [
                hraw[pl.ds((tap // 8) * 256 + block * 64 + tap % 8, 8, stride=8), :] for tap in (2 * i, 2 * i + 1)
            ]
            rows = slice(block * 8, block * 8 + 8)
            hbuf[i, rows, :] = even
            hbuf[HALF + i, rows, :] = odd
            hbuf[2 * HALF + i, rows, :] = even + odd

    def filter_rows(sig, part, block, base):
        rows = slice(block * 8, block * 8 + 8)
        here = pl.ds(block * 16 + sig, 8, stride=2)
        window = vbuf[part, pl.ds(base, FIRST - 1), here, :].astype(jnp.float32).reshape(FIRST // 2, 2, 8, LANES)
        last = vbuf[part, pl.ds(base + FIRST - 1, 1), here, :].astype(jnp.float32)
        even, odd = window[:, 0], window[:, 1]
        ahead = jnp.concatenate([even[1:], last], axis=0)

        def short(which, values):
            total = hbuf[which * HALF, rows, :][None] * values[0 : SB // 2]
            for i in range(1, HALF):
                total = total + hbuf[which * HALF + i, rows, :][None] * values[i : i + SB // 2]
            return total

        shared = short(2, odd)
        first = short(0, even - odd) + shared
        second = short(1, ahead - odd) + shared
        return jnp.stack([first, second], axis=1).reshape(SB, 8, LANES)

    def filter_block(sig, number):
        base = number * SB
        for part in range(2):
            for pair in range(2):
                both = jnp.concatenate([filter_rows(sig, part, 2 * pair + i, base) for i in range(2)], axis=1)
                xs[:, part * 32 + pair * 16 : part * 32 + pair * 16 + 16, :] = both.astype(jnp.bfloat16)
        for half in range(SB // 8):
            right = jnp.concatenate([xs[half * 8 + 4 * q : half * 8 + 4 * q + 4].reshape(256, LANES) for q in range(2)], axis=1)
            out = jnp.dot(dbuf[...], right, preferred_element_type=jnp.float32)
            out = out[:256] + out[256:]
            for q in range(2):
                af[pl.ds(pl.multiple_of((base + half * 8 + 4 * q) * 64, 256), 256), :] = out[:, q * 128 : (q + 1) * 128]

    def send_to(sig, turn, group, to_chan, half):
        pltpu.make_async_remote_copy(
            src_ref=msg.at[(sig * 4 + turn) * C2 + half + 2 * to_chan],
            dst_ref=got.at[sig * 256 + me],
            send_sem=send,
            recv_sem=recv.at[sig * 4 + turn],
            device_id={"chan": to_chan, "tile": half * 4 + group},
            device_id_type=MESH,
        ).start()

    def group_step(sig, turn):
        group = lax.rem(tile + turn, 4)
        for k in range(8):
            c1 = group * 8 + k
            real = af[pl.ds(c1, SPEC, stride=64), :]
            imag = af[pl.ds(R1 + c1, SPEC, stride=64), :]
            right = jnp.concatenate(
                [jnp.concatenate([real, -imag], axis=1), jnp.concatenate([imag, real], axis=1)], axis=0
            ).astype(jnp.bfloat16)
            out = lax.dot_general(wbuf[c1], right, NT, preferred_element_type=jnp.float32)
            sbuf[k * C2 : (k + 1) * C2, :] = out[:C2] + out[C2:]
        for c2 in range(C2):
            msg[(sig * 4 + turn) * C2 + c2] = sbuf[pl.ds(c2, 8, stride=C2), :].astype(jnp.bfloat16)
        halves = [lax.div(tile, 4), 1 - lax.div(tile, 4)]
        for dx in range(2):
            if dx and sig == 0:

                @pl.when(turn == 0)
                def _():
                    pl.semaphore_wait(ready, 7)

            for dh in range(2):
                for dz in Z_ORDER:
                    for dc in range(2):
                        to = functools.partial(send_to, sig, turn, group, chan_at[dz, dh, dc], halves[dx])
                        if dx or dh or dz or dc:
                            to()
                        else:
                            pl.when(turn != 0)(to)

    for sig in range(2):

        def filter_step(number, carry):
            if sig == 0:

                @pl.when(number > 0)
                def _():
                    frames_in(0, number).wait()
                    frames_in(1, number).wait()

            filter_block(sig, number)
            return carry

        def send_step(turn, carry):
            group_step(sig, turn)
            return carry

        if sig == 0:
            frames_in(0, 0).wait()
            frames_in(1, 0).wait()
            first_in.wait()
        lax.fori_loop(0, BLOCKS, filter_step, 0)
        if sig == 0:
            pl.semaphore_wait(barrier, 38)
            for step in range(1, 8):
                signal(ready, chan, tile_at[step])
            second_in.wait()
        lax.fori_loop(0, 4, send_step, 0)
        got[sig * 256 + me] = msg[sig * 256 + 2 * chan + lax.div(tile, 4)]

    to = lax.broadcasted_iota(jnp.int32, (256, 256), 0)
    come = lax.broadcasted_iota(jnp.int32, (256, 256), 1)
    sort = (to == (come % 8) * 32 + (come // 8 % 16) * 2 + come // 128).astype(jnp.bfloat16)

    def out_copy(from_tile, slot):
        where = pl.ds(pl.multiple_of(from_tile * 64, 64), 64)
        return pltpu.make_async_copy(ordered.at[:, where], out_hbm.at[:, where], osem.at[slot])

    for turn in range(4):
        for sig in range(2):
            count = pl.ds(0, 64 if turn else 63)
            pltpu.make_async_copy(msg.at[count], got.at[count], recv.at[sig * 4 + turn]).wait()
        group = lax.rem(tile + 4 - turn, 4)
        for half in range(2):
            from_tile = half * 4 + group
            right = jnp.concatenate(
                [
                    jnp.concatenate(
                        [got[pl.ds(sig * 256 + from_tile * 32 + 16 * q, 16)].reshape(128, LANES) for sig in range(2)], axis=0
                    )
                    for q in range(2)
                ],
                axis=1,
            )
            rows = jnp.dot(sort, right, preferred_element_type=jnp.float32).astype(jnp.bfloat16)
            for q in range(2):
                here = pl.ds(pl.multiple_of(from_tile * 64 + 32 * q, 32), 32)
                ordered[:, here, :] = rows[:, q * 128 : (q + 1) * 128].reshape(8, 32, LANES)
            out_copy(from_tile, turn * 2 + half).start()
    for turn in range(4):
        for half in range(2):
            out_copy(half * 4 + lax.rem(tile + 4 - turn, 4), turn * 2 + half).wait()
    everything = pl.ds(0, 510)
    pltpu.make_async_copy(msg.at[everything], got.at[everything], send).wait()


def correlate(x_hbm, out_hbm, x, out, isem, osem):
    ins = [pltpu.make_async_copy(x_hbm.at[k], x.at[k], isem.at[k]) for k in range(8)]
    outs = [pltpu.make_async_copy(out.at[k], out_hbm.at[k], osem.at[k]) for k in range(8)]
    for copy in ins:
        copy.start()
    upper = lax.broadcasted_iota(jnp.int32, (256, 256), 0) <= lax.broadcasted_iota(jnp.int32, (256, 256), 1)
    for k in range(8):
        ins[k].wait()
        here = x[k]
        wide = here.astype(jnp.float32)
        turned = jnp.concatenate([wide[:, SPEC:], -wide[:, :SPEC]], axis=1).astype(jnp.bfloat16)

        def product(left, lo, hi):
            return lax.dot_general(
                left[lo * 256 : lo * 256 + 256], here[hi * 256 : hi * 256 + 256], NT, preferred_element_type=jnp.float32
            )

        for lo in range(2):
            for hi in range(2):
                if lo < hi:
                    block = product(here, lo, hi)
                elif lo > hi:
                    block = product(turned, lo, hi)
                else:
                    block = jnp.where(upper, product(here, lo, hi), product(turned, lo, hi))
                out[k, lo * 256 : lo * 256 + 256, hi * 256 : hi * 256 + 256] = (block * (1.0 / SPEC)).astype(jnp.bfloat16)
        outs[k].start()
    for copy in outs:
        copy.wait()


def per_device(voltages, filter_taps):
    rows = NFFT // LANES
    frames = voltages.reshape(2, 2, FRAMES * rows, LANES).transpose(0, 2, 1, 3).reshape(2, FRAMES, 2 * rows, LANES)
    taps = filter_taps.reshape(2, 8, rows, LANES).transpose(0, 2, 1, 3).reshape(2 * rows * 8, LANES)
    first, second = first_table(), second_table()
    hbm = pl.BlockSpec(memory_space=pl.ANY)
    dma = pltpu.SemaphoreType.DMA
    ordered = pl.pallas_call(
        channelize,
        name="channelize",
        out_shape=jax.ShapeDtypeStruct((8, 512, LANES), jnp.bfloat16),
        in_specs=[hbm] * 4,
        out_specs=hbm,
        scratch_shapes=[
            pltpu.VMEM((2, FRAMES, 2 * rows, LANES), jnp.int32),
            pltpu.VMEM(taps.shape, jnp.float32),
            pltpu.VMEM((3 * HALF, rows, LANES), jnp.float32),
            pltpu.VMEM(first.shape, jnp.bfloat16),
            pltpu.VMEM(second.shape, jnp.bfloat16),
            pltpu.VMEM((SB, 2 * rows, LANES), jnp.bfloat16),
            pltpu.VMEM((SPEC * 64, LANES), jnp.float32),
            pltpu.VMEM((8 * C2, LANES), jnp.float32),
            pltpu.VMEM((512, 8, LANES), jnp.bfloat16),
            pltpu.VMEM((512, 8, LANES), jnp.bfloat16),
            pltpu.VMEM((8, 512, LANES), jnp.bfloat16),
            dma((2, BLOCKS)),
            dma((3,)),
            dma((8,)),
            dma,
            dma((8,)),
            pltpu.SemaphoreType.REGULAR,
        ],
        compiler_params=pltpu.CompilerParams(collective_id=0, has_side_effects=True, vmem_limit_bytes=60 << 20),
    )(frames, taps, jnp.asarray(first), jnp.asarray(second))
    return pl.pallas_call(
        correlate,
        name="correlate",
        out_shape=jax.ShapeDtypeStruct((8, 512, 512), jnp.bfloat16),
        in_specs=[hbm],
        out_specs=hbm,
        scratch_shapes=[
            pltpu.VMEM((8, 512, LANES), jnp.bfloat16),
            pltpu.VMEM((8, 512, 512), jnp.bfloat16),
            dma((8,)),
            dma((8,)),
        ],
        compiler_params=pltpu.CompilerParams(vmem_limit_bytes=60 << 20),
    )(ordered)


def solution(mesh):
    return jax.shard_map(
        per_device,
        mesh=mesh,
        in_specs=(P(None, ("tile", "chan"), None), P()),
        out_specs=P(("chan", "tile"), None, None),
        check_vma=False,
    )
```

```python
import functools
import math

import jax
import jax.numpy as jnp
import ml_dtypes
import numpy as np
from jax import lax
from jax.experimental import pallas as pl
from jax.experimental.pallas import tpu as pltpu
from jax.sharding import PartitionSpec as P

MESH = pl.DeviceIdType.MESH
NFFT, TAPS, SPEC, KEEP = 4096, 16, 64, 2048
FRAMES = SPEC + TAPS - 1
LANES = 128
R1 = NFFT // LANES
C2 = KEEP // R1
SB = 16
BLOCKS = SPEC // SB
FIRST = SB + TAPS - 1
HALF = TAPS // 2
NT = (((1,), (1,)), ((), ()))


def split(values):
    high = values.astype(ml_dtypes.bfloat16)
    low = (values - high.astype(np.float64)).astype(ml_dtypes.bfloat16)
    return high, low


@functools.cache
def first_table():
    c1, j = np.meshgrid(np.arange(R1), np.arange(R1), indexing="ij")
    angle = 2 * math.pi * ((c1 * j) % R1) / R1
    cos, sin = np.cos(angle), np.sin(angle)
    unit = np.concatenate([np.concatenate([cos, sin], 1), np.concatenate([-sin, cos], 1)], 0)
    return np.concatenate(split(np.kron(np.eye(2), unit)), 1)


@functools.cache
def second_table():
    chan = np.arange(R1)[:, None, None] + R1 * np.arange(C2)[None, :, None]
    angle = 2 * math.pi * ((chan * np.arange(LANES)) % NFFT) / NFFT
    full = np.concatenate([np.cos(angle), -np.sin(angle)], 2) / (math.sqrt(NFFT) * math.sqrt(SPEC))
    return np.concatenate(split(full), 1)


Z_ORDER = (4, 3, 5, 2, 6, 1, 7, 0)


def chan_table():
    chan = lax.axis_index("chan")
    z, high, core = lax.div(chan, 4), lax.rem(lax.div(chan, 2), 2), lax.rem(chan, 2)
    z_part = [lax.rem(z + dz, 8) * 4 for dz in range(8)]
    y_part = [high * 2, 2 - high * 2]
    c_part = [core, 1 - core]
    return chan, {(dz, dh, dc): z_part[dz] + (y_part[dh] + c_part[dc]) for dz in range(8) for dh in range(2) for dc in range(2)}


def signal(sem, chan, tile):
    pl.semaphore_signal(sem, inc=1, device_id={"chan": chan, "tile": tile}, device_id_type=MESH)


def channelize(v_hbm, hraw, t_hbm, ordered, vbuf, hbuf, dbuf, wbuf, xs, af, sbuf, msg, got, vsem, csem, send, recv, ready):
    barrier = pltpu.get_barrier_semaphore()
    chan, chan_at = chan_table()
    tile = lax.axis_index("tile")
    tile_at = [lax.rem(tile + step, 8) for step in range(8)]
    me = tile * 32 + chan

    def frames_in(part, chunk):
        where = pl.ds(0, FIRST) if isinstance(chunk, int) and chunk == 0 else pl.ds(chunk * SB + TAPS - 1, SB)
        return pltpu.make_async_copy(v_hbm.at[part, where], vbuf.at[part, where], vsem.at[part, chunk])

    first_in = pltpu.make_async_copy(t_hbm.at[R1], dbuf, csem.at[0])
    second_in = pltpu.make_async_copy(t_hbm.at[pl.ds(0, R1)], wbuf, csem.at[1])
    frames_in(0, 0).start()
    frames_in(1, 0).start()
    first_in.start()
    for chunk in range(1, BLOCKS):
        for part in range(2):
            frames_in(part, chunk).start()
    second_in.start()

    for dz in Z_ORDER:
        for dx in range(2):
            for dh in range(2):
                for dc in range(2):
                    if dz or dx or dh or dc:
                        signal(barrier, chan_at[dz, dh, dc], tile_at[4 * dx])
    for turn in range(1, 4):
        signal(barrier, chan, tile_at[turn])

    for block in range(4):
        for i in range(HALF):
            even, odd = [
                hraw[pl.ds((tap // 8) * 256 + block * 64 + tap % 8, 8, stride=8), :] for tap in (2 * i, 2 * i + 1)
            ]
            rows = slice(block * 8, block * 8 + 8)
            hbuf[i, rows, :] = even
            hbuf[HALF + i, rows, :] = odd
            hbuf[2 * HALF + i, rows, :] = even + odd

    def filter_rows(sig, part, block, base):
        rows = slice(block * 8, block * 8 + 8)
        here = pl.ds(block * 16 + sig, 8, stride=2)
        window = vbuf[part, pl.ds(base, FIRST - 1), here, :].astype(jnp.float32).reshape(FIRST // 2, 2, 8, LANES)
        last = vbuf[part, pl.ds(base + FIRST - 1, 1), here, :].astype(jnp.float32)
        even, odd = window[:, 0], window[:, 1]
        ahead = jnp.concatenate([even[1:], last], axis=0)

        def short(which, values):
            total = hbuf[which * HALF, rows, :][None] * values[0 : SB // 2]
            for i in range(1, HALF):
                total = total + hbuf[which * HALF + i, rows, :][None] * values[i : i + SB // 2]
            return total

        shared = short(2, odd)
        first = short(0, even - odd) + shared
        second = short(1, ahead - odd) + shared
        return jnp.stack([first, second], axis=1).reshape(SB, 8, LANES)

    def filter_block(sig, number):
        base = number * SB
        for part in range(2):
            for pair in range(2):
                both = jnp.concatenate([filter_rows(sig, part, 2 * pair + i, base) for i in range(2)], axis=1)
                xs[:, part * 32 + pair * 16 : part * 32 + pair * 16 + 16, :] = both.astype(jnp.bfloat16)
        for quad in range(SB // 4):
            pairs = [xs[quad * 4 + 2 * q : quad * 4 + 2 * q + 2].reshape(128, LANES) for q in range(2)]
            right = jnp.concatenate([jnp.concatenate([pair, pair], axis=0) for pair in pairs], axis=1)
            out = jnp.dot(dbuf[...], right, preferred_element_type=jnp.float32)
            for q in range(2):
                af[pl.ds(pl.multiple_of((base + quad * 4 + 2 * q) * 64, 128), 128), :] = out[:, q * 128 : (q + 1) * 128]

    def send_to(sig, turn, group, to_chan, half):
        pltpu.make_async_remote_copy(
            src_ref=msg.at[(sig * 4 + turn) * C2 + half + 2 * to_chan],
            dst_ref=got.at[sig * 256 + me],
            send_sem=send,
            recv_sem=recv.at[sig * 4 + turn],
            device_id={"chan": to_chan, "tile": half * 4 + group},
            device_id_type=MESH,
        ).start()

    def group_step(sig, turn):
        group = lax.rem(tile + turn, 4)
        for k in range(8):
            c1 = group * 8 + k
            real = af[pl.ds(c1, SPEC, stride=64), :]
            imag = af[pl.ds(R1 + c1, SPEC, stride=64), :]
            right = jnp.concatenate(
                [jnp.concatenate([real, -imag], axis=1), jnp.concatenate([imag, real], axis=1)], axis=0
            ).astype(jnp.bfloat16)
            out = lax.dot_general(wbuf[c1], right, NT, preferred_element_type=jnp.float32)
            sbuf[k * C2 : (k + 1) * C2, :] = out[:C2] + out[C2:]
        for c2 in range(C2):
            msg[(sig * 4 + turn) * C2 + c2] = sbuf[pl.ds(c2, 8, stride=C2), :].astype(jnp.bfloat16)
        if sig == 0:

            @pl.when(turn > 0)
            def _():
                pl.semaphore_wait(ready.at[turn], 1)

        halves = [lax.div(tile, 4), 1 - lax.div(tile, 4)]
        for dx in range(2):
            for dh in range(2):
                for dz in Z_ORDER:
                    for dc in range(2):
                        to = functools.partial(send_to, sig, turn, group, chan_at[dz, dh, dc], halves[dx])
                        if dx or dh or dz or dc:
                            to()
                        else:
                            pl.when(turn != 0)(to)

    for sig in range(2):

        def filter_step(number, carry):
            if sig == 0:

                @pl.when(number > 0)
                def _():
                    frames_in(0, number).wait()
                    frames_in(1, number).wait()

            filter_block(sig, number)
            return carry

        def send_step(turn, carry):
            group_step(sig, turn)
            return carry

        if sig == 0:
            frames_in(0, 0).wait()
            frames_in(1, 0).wait()
            first_in.wait()
        lax.fori_loop(0, BLOCKS, filter_step, 0)
        if sig == 0:
            pl.semaphore_wait(barrier, 66)
            for turn in range(1, 4):
                signal(ready.at[turn], chan, tile_at[8 - turn])
            second_in.wait()
        lax.fori_loop(0, 4, send_step, 0)
        got[sig * 256 + me] = msg[sig * 256 + 2 * chan + lax.div(tile, 4)]

    to = lax.broadcasted_iota(jnp.int32, (256, 256), 0)
    come = lax.broadcasted_iota(jnp.int32, (256, 256), 1)
    sort = (to == (come % 8) * 32 + (come // 8 % 16) * 2 + come // 128).astype(jnp.bfloat16)

    for turn in range(4):
        for sig in range(2):
            count = pl.ds(0, 64 if turn else 63)
            pltpu.make_async_copy(msg.at[count], got.at[count], recv.at[sig * 4 + turn]).wait()
        group = lax.rem(tile + 4 - turn, 4)
        for half in range(2):
            from_tile = half * 4 + group
            right = jnp.concatenate(
                [
                    jnp.concatenate(
                        [got[pl.ds(sig * 256 + from_tile * 32 + 16 * q, 16)].reshape(128, LANES) for sig in range(2)], axis=0
                    )
                    for q in range(2)
                ],
                axis=1,
            )
            rows = jnp.dot(sort, right, preferred_element_type=jnp.float32)
            for q in range(2):
                here = pl.ds(pl.multiple_of(from_tile * 64 + 32 * q, 32), 32)
                part = rows[:, q * 128 : (q + 1) * 128]
                ordered[:, here, :] = part.astype(jnp.bfloat16).reshape(8, 32, LANES)
    everything = pl.ds(0, 510)
    pltpu.make_async_copy(msg.at[everything], got.at[everything], send).wait()


def correlate(x, out_hbm, out, osem):
    outs = [pltpu.make_async_copy(out.at[k], out_hbm.at[k], osem.at[k]) for k in range(8)]
    upper = lax.broadcasted_iota(jnp.int32, (256, 256), 0) <= lax.broadcasted_iota(jnp.int32, (256, 256), 1)
    for k in range(8):
        here = x[k]
        wide = here.astype(jnp.float32)
        turned = jnp.concatenate([wide[:, SPEC:], -wide[:, :SPEC]], axis=1).astype(jnp.bfloat16)

        def product(imag, lo, hi):
            left = (turned if imag else here)[lo * 256 : lo * 256 + 256]
            return lax.dot_general(left, here[hi * 256 : hi * 256 + 256], NT, preferred_element_type=jnp.float32)

        for lo in range(2):
            for hi in range(2):
                if lo != hi:
                    block = product(int(lo > hi), lo, hi)
                else:
                    block = jnp.where(upper, product(0, lo, hi), product(1, lo, hi))
                out[k, lo * 256 : lo * 256 + 256, hi * 256 : hi * 256 + 256] = block.astype(jnp.bfloat16)
        outs[k].start()
    for copy in outs:
        copy.wait()


def per_device(voltages, filter_taps):
    rows = NFFT // LANES
    frames = voltages.reshape(2, 2, FRAMES * rows, LANES).transpose(0, 2, 1, 3).reshape(2, FRAMES, 2 * rows, LANES)
    taps = filter_taps.reshape(2, 8, rows, LANES).transpose(0, 2, 1, 3).reshape(2 * rows * 8, LANES)
    tables = np.concatenate([second_table(), first_table()[None]], 0)
    hbm, vmem = pl.BlockSpec(memory_space=pl.ANY), pl.BlockSpec(memory_space=pltpu.VMEM)
    dma = pltpu.SemaphoreType.DMA
    ordered = pl.pallas_call(
        channelize,
        name="channelize",
        out_shape=jax.ShapeDtypeStruct((8, 512, LANES), jnp.bfloat16),
        in_specs=[hbm, vmem, hbm],
        out_specs=vmem,
        scratch_shapes=[
            pltpu.VMEM((2, FRAMES, 2 * rows, LANES), jnp.int32),
            pltpu.VMEM((3 * HALF, rows, LANES), jnp.float32),
            pltpu.VMEM(tables.shape[1:], jnp.bfloat16),
            pltpu.VMEM((R1,) + tables.shape[1:], jnp.bfloat16),
            pltpu.VMEM((SB, 2 * rows, LANES), jnp.bfloat16),
            pltpu.VMEM((SPEC * 64, LANES), jnp.float32),
            pltpu.VMEM((8 * C2, LANES), jnp.float32),
            pltpu.VMEM((512, 8, LANES), jnp.bfloat16),
            pltpu.VMEM((512, 8, LANES), jnp.bfloat16),
            dma((2, BLOCKS)),
            dma((2,)),
            dma,
            dma((8,)),
            pltpu.SemaphoreType.REGULAR((4,)),
        ],
        compiler_params=pltpu.CompilerParams(collective_id=0, has_side_effects=True, vmem_limit_bytes=52 << 20),
    )(frames, taps, jnp.asarray(tables))
    return pl.pallas_call(
        correlate,
        name="correlate",
        out_shape=jax.ShapeDtypeStruct((8, 512, 512), jnp.bfloat16),
        in_specs=[vmem],
        out_specs=hbm,
        scratch_shapes=[
            pltpu.VMEM((8, 512, 512), jnp.bfloat16),
            dma((8,)),
        ],
        compiler_params=pltpu.CompilerParams(vmem_limit_bytes=48 << 20),
    )(ordered)


def solution(mesh):
    return jax.shard_map(
        per_device,
        mesh=mesh,
        in_specs=(P(None, ("tile", "chan"), None), P()),
        out_specs=P(("chan", "tile"), None, None),
        check_vma=False,
    )
```

```python
import functools
import math

import jax
import jax.numpy as jnp
import ml_dtypes
import numpy as np
from jax import lax
from jax.experimental import pallas as pl
from jax.experimental.pallas import tpu as pltpu
from jax.sharding import PartitionSpec as P

MESH = pl.DeviceIdType.MESH
NFFT, TAPS, SPEC, KEEP = 4096, 16, 64, 2048
FRAMES = SPEC + TAPS - 1
LANES = 128
R1 = NFFT // LANES
C2 = KEEP // R1
SB = 16
BLOCKS = SPEC // SB
FIRST = SB + TAPS - 1
HALF = TAPS // 2
NT = (((1,), (1,)), ((), ()))


def split(values):
    high = values.astype(ml_dtypes.bfloat16)
    low = (values - high.astype(np.float64)).astype(ml_dtypes.bfloat16)
    return high, low


@functools.cache
def first_table():
    c1, j = np.meshgrid(np.arange(R1), np.arange(R1), indexing="ij")
    angle = 2 * math.pi * ((c1 * j) % R1) / R1
    cos, sin = np.cos(angle), np.sin(angle)
    unit = np.concatenate([np.concatenate([cos, sin], 1), np.concatenate([-sin, cos], 1)], 0)
    return np.concatenate(split(np.kron(np.eye(2), unit)), 1)


@functools.cache
def second_table():
    chan = np.arange(R1)[:, None, None] + R1 * np.arange(C2)[None, :, None]
    angle = 2 * math.pi * ((chan * np.arange(LANES)) % NFFT) / NFFT
    full = np.concatenate([np.cos(angle), -np.sin(angle)], 2) / (math.sqrt(NFFT) * math.sqrt(SPEC))
    return np.concatenate(split(full), 1)


Z_ORDER = (4, 3, 5, 2, 6, 1, 7, 0)


def chan_table():
    chan = lax.axis_index("chan")
    z, high, core = lax.div(chan, 4), lax.rem(lax.div(chan, 2), 2), lax.rem(chan, 2)
    z_part = [lax.rem(z + dz, 8) * 4 for dz in range(8)]
    y_part = [high * 2, 2 - high * 2]
    c_part = [core, 1 - core]
    return chan, {(dz, dh, dc): z_part[dz] + (y_part[dh] + c_part[dc]) for dz in range(8) for dh in range(2) for dc in range(2)}


def far_first():
    def hops(to):
        dz, dx, low, high, _ = to
        return min(dz, 8 - dz) + min(dx, 4 - dx) + (1 if low else 2 * high)

    every = [(dz, dx, low, high, dc) for dx in range(4) for low in range(2) for high in range(2) for dz in Z_ORDER for dc in range(2)]
    every = sorted((to for to in every if any(to)), key=lambda to: -hops(to))
    across, within = [to for to in every if to[0]], [to for to in every if not to[0]]
    order = []
    for i, to in enumerate(across):
        order.append(to)
        if i % 5 == 1 and within:
            order.append(within.pop(0))
    return order + within


def signal(sem, chan, tile):
    pl.semaphore_signal(sem, inc=1, device_id={"chan": chan, "tile": tile}, device_id_type=MESH)


def channelize(v_hbm, hraw, t_hbm, ordered, vbuf, hbuf, dbuf, wbuf, xs, af, sbuf, msg, got, vsem, csem, send, recv, ready):
    barrier = pltpu.get_barrier_semaphore()
    chan, chan_at = chan_table()
    tile = lax.axis_index("tile")
    tile_at = [lax.rem(tile + step, 8) for step in range(8)]
    me = tile * 32 + chan

    def frames_in(part, chunk):
        where = pl.ds(0, FIRST) if isinstance(chunk, int) and chunk == 0 else pl.ds(chunk * SB + TAPS - 1, SB)
        return pltpu.make_async_copy(v_hbm.at[part, where], vbuf.at[part, where], vsem.at[part, chunk])

    first_in = pltpu.make_async_copy(t_hbm.at[R1], dbuf, csem.at[0])
    second_in = pltpu.make_async_copy(t_hbm.at[pl.ds(0, R1)], wbuf, csem.at[1])
    frames_in(0, 0).start()
    frames_in(1, 0).start()
    first_in.start()
    for chunk in range(1, BLOCKS):
        for part in range(2):
            frames_in(part, chunk).start()
    second_in.start()

    for dz in Z_ORDER:
        for dx in range(2):
            for dh in range(2):
                for dc in range(2):
                    if dz or dx or dh or dc:
                        signal(barrier, chan_at[dz, dh, dc], tile_at[4 * dx])
    for turn in range(1, 4):
        signal(barrier, chan, tile_at[turn])

    for block in range(4):
        for i in range(HALF):
            even, odd = [
                hraw[pl.ds((tap // 8) * 256 + block * 64 + tap % 8, 8, stride=8), :] for tap in (2 * i, 2 * i + 1)
            ]
            rows = slice(block * 8, block * 8 + 8)
            hbuf[i, rows, :] = even
            hbuf[HALF + i, rows, :] = odd
            hbuf[2 * HALF + i, rows, :] = even + odd

    def filter_rows(sig, part, block, base):
        rows = slice(block * 8, block * 8 + 8)
        here = pl.ds(block * 16 + sig, 8, stride=2)
        window = vbuf[part, pl.ds(base, FIRST - 1), here, :].astype(jnp.float32).reshape(FIRST // 2, 2, 8, LANES)
        last = vbuf[part, pl.ds(base + FIRST - 1, 1), here, :].astype(jnp.float32)
        even, odd = window[:, 0], window[:, 1]
        ahead = jnp.concatenate([even[1:], last], axis=0)

        def short(which, values):
            total = hbuf[which * HALF, rows, :][None] * values[0 : SB // 2]
            for i in range(1, HALF):
                total = total + hbuf[which * HALF + i, rows, :][None] * values[i : i + SB // 2]
            return total

        shared = short(2, odd)
        first = short(0, even - odd) + shared
        second = short(1, ahead - odd) + shared
        return jnp.stack([first, second], axis=1).reshape(SB, 8, LANES)

    def filter_block(sig, number):
        base = number * SB
        for part in range(2):
            for pair in range(2):
                both = jnp.concatenate([filter_rows(sig, part, 2 * pair + i, base) for i in range(2)], axis=1)
                xs[:, part * 32 + pair * 16 : part * 32 + pair * 16 + 16, :] = both.astype(jnp.bfloat16)
        for quad in range(SB // 4):
            pairs = [xs[quad * 4 + 2 * q : quad * 4 + 2 * q + 2].reshape(128, LANES) for q in range(2)]
            right = jnp.concatenate([jnp.concatenate([pair, pair], axis=0) for pair in pairs], axis=1)
            out = jnp.dot(dbuf[...], right, preferred_element_type=jnp.float32)
            for q in range(2):
                af[pl.ds(pl.multiple_of((base + quad * 4 + 2 * q) * 64, 128), 128), :] = out[:, q * 128 : (q + 1) * 128]

    def send_to(sig, place, to_chan, to_tile):
        pltpu.make_async_remote_copy(
            src_ref=msg.at[place + 2 * to_chan],
            dst_ref=got.at[sig * 256 + me],
            send_sem=send,
            recv_sem=recv.at[sig],
            device_id={"chan": to_chan, "tile": to_tile},
            device_id_type=MESH,
        ).start()

    def transform(sig, group):
        for k in range(8):
            c1 = group * 8 + k
            real = af[pl.ds(c1, SPEC, stride=64), :]
            imag = af[pl.ds(R1 + c1, SPEC, stride=64), :]
            right = jnp.concatenate(
                [jnp.concatenate([real, -imag], axis=1), jnp.concatenate([imag, real], axis=1)], axis=0
            ).astype(jnp.bfloat16)
            out = lax.dot_general(wbuf[c1], right, NT, preferred_element_type=jnp.float32)
            sbuf[k * C2 : (k + 1) * C2, :] = out[:C2] + out[C2:]
        for c2 in range(C2):
            msg[(sig * 4 + group) * C2 + c2] = sbuf[pl.ds(c2, 8, stride=C2), :].astype(jnp.bfloat16)

    def first_sends(turn, carry):
        group = lax.rem(tile + turn, 4)
        transform(0, group)

        @pl.when(turn > 0)
        def _():
            pl.semaphore_wait(ready.at[turn], 1)

        own_half = lax.div(tile, 4)
        for dx in range(2):
            half = 1 - own_half if dx else own_half
            for dh in range(2):
                for dz in Z_ORDER:
                    for dc in range(2):
                        to = functools.partial(send_to, 0, group * C2 + half, chan_at[dz, dh, dc], half * 4 + group)
                        if dx or dh or dz or dc:
                            to()
                        else:
                            pl.when(turn != 0)(to)
        return carry

    def second_sends():
        x, low = lax.div(tile, 2), lax.rem(tile, 2)
        x_at = [lax.rem(x + dx, 4) for dx in range(4)]
        low_at = [low, 1 - low]
        tiles = {(dx, dl): x_at[dx] * 2 + low_at[dl] for dx in range(4) for dl in range(2)}
        places = {to: (4 + lax.rem(at, 4)) * C2 + lax.div(at, 4) for to, at in tiles.items()}
        for dz, dx, dl, dh, dc in far_first():
            send_to(1, places[dx, dl], chan_at[dz, dh, dc], tiles[dx, dl])

    for sig in range(2):

        def filter_step(number, carry):
            if sig == 0:

                @pl.when(number > 0)
                def _():
                    frames_in(0, number).wait()
                    frames_in(1, number).wait()

            filter_block(sig, number)
            return carry

        def transform_step(group, carry):
            transform(1, group)
            return carry

        if sig == 0:
            frames_in(0, 0).wait()
            frames_in(1, 0).wait()
            first_in.wait()
        lax.fori_loop(0, BLOCKS, filter_step, 0)
        if sig == 0:
            pl.semaphore_wait(barrier, 66)
            for turn in range(1, 4):
                signal(ready.at[turn], chan, tile_at[8 - turn])
            second_in.wait()
            lax.fori_loop(0, 4, first_sends, 0)
        else:
            lax.fori_loop(0, 4, transform_step, 0)
            second_sends()
        got[sig * 256 + me] = msg[(sig * 4 + lax.rem(tile, 4)) * C2 + 2 * chan + lax.div(tile, 4)]

    to = lax.broadcasted_iota(jnp.int32, (256, 256), 0)
    come = lax.broadcasted_iota(jnp.int32, (256, 256), 1)
    sort = (to == (come % 8) * 32 + (come // 8 % 16) * 2 + come // 128).astype(jnp.bfloat16)

    others = pl.ds(0, 255)
    for sig in range(2):
        pltpu.make_async_copy(msg.at[others], got.at[others], recv.at[sig]).wait()
    for from_tile in range(8):
        right = jnp.concatenate(
            [
                jnp.concatenate(
                    [got[sig * 256 + from_tile * 32 + 16 * q : sig * 256 + from_tile * 32 + 16 * q + 16].reshape(128, LANES) for sig in range(2)], axis=0
                )
                for q in range(2)
            ],
            axis=1,
        )
        rows = jnp.dot(sort, right, preferred_element_type=jnp.float32)
        for q in range(2):
            here = slice(from_tile * 64 + 32 * q, from_tile * 64 + 32 * q + 32)
            part = rows[:, q * 128 : (q + 1) * 128]
            ordered[:, here, :] = part.astype(jnp.bfloat16).reshape(8, 32, LANES)
    everything = pl.ds(0, 510)
    pltpu.make_async_copy(msg.at[everything], got.at[everything], send).wait()


def correlate(x, out_hbm, out, osem):
    outs = [pltpu.make_async_copy(out.at[k], out_hbm.at[k], osem.at[k]) for k in range(8)]
    upper = lax.broadcasted_iota(jnp.int32, (256, 256), 0) <= lax.broadcasted_iota(jnp.int32, (256, 256), 1)
    for k in range(8):
        here = x[k]
        wide = here.astype(jnp.float32)
        turned = jnp.concatenate([wide[:, SPEC:], -wide[:, :SPEC]], axis=1).astype(jnp.bfloat16)

        def product(imag, lo, hi):
            left = (turned if imag else here)[lo * 256 : lo * 256 + 256]
            return lax.dot_general(left, here[hi * 256 : hi * 256 + 256], NT, preferred_element_type=jnp.float32)

        for lo in range(2):
            for hi in range(2):
                if lo != hi:
                    block = product(int(lo > hi), lo, hi)
                else:
                    block = jnp.where(upper, product(0, lo, hi), product(1, lo, hi))
                out[k, lo * 256 : lo * 256 + 256, hi * 256 : hi * 256 + 256] = block.astype(jnp.bfloat16)
        outs[k].start()
    for copy in outs:
        copy.wait()


def per_device(voltages, filter_taps):
    rows = NFFT // LANES
    frames = voltages.reshape(2, 2, FRAMES * rows, LANES).transpose(0, 2, 1, 3).reshape(2, FRAMES, 2 * rows, LANES)
    taps = filter_taps.reshape(2, 8, rows, LANES).transpose(0, 2, 1, 3).reshape(2 * rows * 8, LANES)
    tables = np.concatenate([second_table(), first_table()[None]], 0)
    hbm, vmem = pl.BlockSpec(memory_space=pl.ANY), pl.BlockSpec(memory_space=pltpu.VMEM)
    dma = pltpu.SemaphoreType.DMA
    ordered = pl.pallas_call(
        channelize,
        name="channelize",
        out_shape=jax.ShapeDtypeStruct((8, 512, LANES), jnp.bfloat16),
        in_specs=[hbm, vmem, hbm],
        out_specs=vmem,
        scratch_shapes=[
            pltpu.VMEM((2, FRAMES, 2 * rows, LANES), jnp.int32),
            pltpu.VMEM((3 * HALF, rows, LANES), jnp.float32),
            pltpu.VMEM(tables.shape[1:], jnp.bfloat16),
            pltpu.VMEM((R1,) + tables.shape[1:], jnp.bfloat16),
            pltpu.VMEM((SB, 2 * rows, LANES), jnp.bfloat16),
            pltpu.VMEM((SPEC * 64, LANES), jnp.float32),
            pltpu.VMEM((8 * C2, LANES), jnp.float32),
            pltpu.VMEM((512, 8, LANES), jnp.bfloat16),
            pltpu.VMEM((512, 8, LANES), jnp.bfloat16),
            dma((2, BLOCKS)),
            dma((2,)),
            dma,
            dma((2,)),
            pltpu.SemaphoreType.REGULAR((4,)),
        ],
        compiler_params=pltpu.CompilerParams(collective_id=0, has_side_effects=True, vmem_limit_bytes=52 << 20),
    )(frames, taps, jnp.asarray(tables))
    return pl.pallas_call(
        correlate,
        name="correlate",
        out_shape=jax.ShapeDtypeStruct((8, 512, 512), jnp.bfloat16),
        in_specs=[vmem],
        out_specs=hbm,
        scratch_shapes=[
            pltpu.VMEM((8, 512, 512), jnp.bfloat16),
            dma((8,)),
        ],
        compiler_params=pltpu.CompilerParams(vmem_limit_bytes=48 << 20),
    )(ordered)


def solution(mesh):
    return jax.shard_map(
        per_device,
        mesh=mesh,
        in_specs=(P(None, ("tile", "chan"), None), P()),
        out_specs=P(("chan", "tile"), None, None),
        check_vma=False,
    )
```

```python
import functools
import math

import jax
import jax.numpy as jnp
import ml_dtypes
import numpy as np
from jax import lax
from jax.experimental import pallas as pl
from jax.experimental.pallas import tpu as pltpu
from jax.sharding import PartitionSpec as P

MESH = pl.DeviceIdType.MESH
NFFT, TAPS, SPEC, KEEP = 4096, 16, 64, 2048
FRAMES = SPEC + TAPS - 1
LANES = 128
R1 = NFFT // LANES
C2 = KEEP // R1
SB = 16
BLOCKS = SPEC // SB
FIRST = SB + TAPS - 1
HALF = TAPS // 2
NT = (((1,), (1,)), ((), ()))


def split(values):
    high = values.astype(ml_dtypes.bfloat16)
    low = (values - high.astype(np.float64)).astype(ml_dtypes.bfloat16)
    return high, low


@functools.cache
def first_table():
    c1, j = np.meshgrid(np.arange(R1), np.arange(R1), indexing="ij")
    angle = 2 * math.pi * ((c1 * j) % R1) / R1
    cos, sin = np.cos(angle), np.sin(angle)
    unit = np.concatenate([np.concatenate([cos, sin], 1), np.concatenate([-sin, cos], 1)], 0)
    return np.concatenate(split(np.kron(np.eye(2), unit)), 1)


@functools.cache
def second_table():
    chan = np.arange(R1)[:, None, None] + R1 * np.arange(C2)[None, :, None]
    angle = 2 * math.pi * ((chan * np.arange(LANES)) % NFFT) / NFFT
    full = np.concatenate([np.cos(angle), -np.sin(angle)], 2) / (math.sqrt(NFFT) * math.sqrt(SPEC))
    return np.concatenate(split(full), 1)


Z_ORDER = (4, 3, 5, 2, 6, 1, 7, 0)


def chan_table():
    chan = lax.axis_index("chan")
    z, high, core = lax.div(chan, 4), lax.rem(lax.div(chan, 2), 2), lax.rem(chan, 2)
    z_part = [lax.rem(z + dz, 8) * 4 for dz in range(8)]
    y_part = [high * 2, 2 - high * 2]
    c_part = [core, 1 - core]
    return chan, {(dz, dh, dc): z_part[dz] + (y_part[dh] + c_part[dc]) for dz in range(8) for dh in range(2) for dc in range(2)}


def far_first():
    def hops(to):
        dz, dx, low, high, _ = to
        return min(dz, 8 - dz) + min(dx, 4 - dx) + (1 if low else 2 * high)

    every = [(dz, dx, low, high, dc) for dx in range(4) for low in range(2) for high in range(2) for dz in Z_ORDER for dc in range(2)]
    every = sorted((to for to in every if any(to)), key=lambda to: -hops(to))
    across, within = [to for to in every if to[0]], [to for to in every if not to[0]]
    order = []
    for i, to in enumerate(across):
        order.append(to)
        if i % 5 == 1 and within:
            order.append(within.pop(0))
    return order + within


def signal(sem, chan, tile):
    pl.semaphore_signal(sem, inc=1, device_id={"chan": chan, "tile": tile}, device_id_type=MESH)


def channelize(v_hbm, hraw, t_hbm, ordered, vbuf, hbuf, dbuf, wbuf, xs, af, sbuf, msg, got, vsem, csem, send, recv, ready):
    barrier = pltpu.get_barrier_semaphore()
    chan, chan_at = chan_table()
    tile = lax.axis_index("tile")
    tile_at = [lax.rem(tile + step, 8) for step in range(8)]
    me = tile * 32 + chan

    def frames_in(part, chunk):
        where = pl.ds(0, FIRST) if isinstance(chunk, int) and chunk == 0 else pl.ds(chunk * SB + TAPS - 1, SB)
        return pltpu.make_async_copy(v_hbm.at[part, where], vbuf.at[part, where], vsem.at[part, chunk])

    first_in = pltpu.make_async_copy(t_hbm.at[R1], dbuf, csem.at[0])
    second_in = pltpu.make_async_copy(t_hbm.at[pl.ds(0, R1)], wbuf, csem.at[1])
    frames_in(0, 0).start()
    frames_in(1, 0).start()
    first_in.start()
    frames_in(0, 1).start()
    frames_in(1, 1).start()

    for dz in Z_ORDER:
        for dx in range(2):
            for dh in range(2):
                for dc in range(2):
                    if dz or dx or dh or dc:
                        signal(barrier, chan_at[dz, dh, dc], tile_at[4 * dx])
    for turn in range(1, 4):
        signal(barrier, chan, tile_at[turn])

    for block in range(4):
        for i in range(HALF):
            even, odd = [
                hraw[pl.ds((tap // 8) * 256 + block * 64 + tap % 8, 8, stride=8), :] for tap in (2 * i, 2 * i + 1)
            ]
            rows = slice(block * 8, block * 8 + 8)
            hbuf[i, rows, :] = even
            hbuf[HALF + i, rows, :] = odd
            hbuf[2 * HALF + i, rows, :] = even + odd

    def filter_rows(sig, part, block, base):
        rows = slice(block * 8, block * 8 + 8)
        here = pl.ds(block * 16 + sig, 8, stride=2)
        window = vbuf[part, pl.ds(base, FIRST - 1), here, :].astype(jnp.float32).reshape(FIRST // 2, 2, 8, LANES)
        last = vbuf[part, pl.ds(base + FIRST - 1, 1), here, :].astype(jnp.float32)
        even, odd = window[:, 0], window[:, 1]
        ahead = jnp.concatenate([even[1:], last], axis=0)

        def short(which, values):
            total = hbuf[which * HALF, rows, :][None] * values[0 : SB // 2]
            for i in range(1, HALF):
                total = total + hbuf[which * HALF + i, rows, :][None] * values[i : i + SB // 2]
            return total

        shared = short(2, odd)
        first = short(0, even - odd) + shared
        second = short(1, ahead - odd) + shared
        return jnp.stack([first, second], axis=1).reshape(SB, 8, LANES)

    def first_stage(number, slot, quad):
        pairs = [xs[slot, quad * 4 + 2 * q : quad * 4 + 2 * q + 2].reshape(128, LANES) for q in range(2)]
        right = jnp.concatenate([jnp.concatenate([pair, pair], axis=0) for pair in pairs], axis=1)
        out = jnp.dot(dbuf[...], right, preferred_element_type=jnp.float32)
        for q in range(2):
            where = pl.ds(pl.multiple_of((number * SB + quad * 4 + 2 * q) * 64, 128), 128)
            af[where, :] = out[:, q * 128 : (q + 1) * 128]

    def filter_block(sig, number, slot, before=None):
        base = number * SB
        for part in range(2):
            for pair in range(2):
                if before is not None:
                    first_stage(before, 1 - slot, part * 2 + pair)
                both = jnp.concatenate([filter_rows(sig, part, 2 * pair + i, base) for i in range(2)], axis=1)
                xs[slot, :, part * 32 + pair * 16 : part * 32 + pair * 16 + 16, :] = both.astype(jnp.bfloat16)

    def send_to(sig, place, to_chan, to_tile):
        pltpu.make_async_remote_copy(
            src_ref=msg.at[place + 2 * to_chan],
            dst_ref=got.at[sig * 256 + me],
            send_sem=send,
            recv_sem=recv.at[sig],
            device_id={"chan": to_chan, "tile": to_tile},
            device_id_type=MESH,
        ).start()

    def transform(sig, group):
        for k in range(8):
            c1 = group * 8 + k
            real = af[pl.ds(c1, SPEC, stride=64), :]
            imag = af[pl.ds(R1 + c1, SPEC, stride=64), :]
            right = jnp.concatenate(
                [jnp.concatenate([real, -imag], axis=1), jnp.concatenate([imag, real], axis=1)], axis=0
            ).astype(jnp.bfloat16)
            out = lax.dot_general(wbuf[c1], right, NT, preferred_element_type=jnp.float32)
            sbuf[k * C2 : (k + 1) * C2, :] = out[:C2] + out[C2:]
        for c2 in range(C2):
            msg[(sig * 4 + group) * C2 + c2] = sbuf[pl.ds(c2, 8, stride=C2), :].astype(jnp.bfloat16)

    def first_sends(turn, carry):
        group = lax.rem(tile + turn, 4)
        transform(0, group)

        @pl.when(turn > 0)
        def _():
            pl.semaphore_wait(ready.at[turn], 1)

        own_half = lax.div(tile, 4)
        for dx in range(2):
            half = 1 - own_half if dx else own_half
            for dh in range(2):
                for dz in Z_ORDER:
                    for dc in range(2):
                        to = functools.partial(send_to, 0, group * C2 + half, chan_at[dz, dh, dc], half * 4 + group)
                        if dx or dh or dz or dc:
                            to()
                        else:
                            pl.when(turn != 0)(to)
        return carry

    def second_sends():
        x, low = lax.div(tile, 2), lax.rem(tile, 2)
        x_at = [lax.rem(x + dx, 4) for dx in range(4)]
        low_at = [low, 1 - low]
        tiles = {(dx, dl): x_at[dx] * 2 + low_at[dl] for dx in range(4) for dl in range(2)}
        places = {to: (4 + lax.rem(at, 4)) * C2 + lax.div(at, 4) for to, at in tiles.items()}
        for dz, dx, dl, dh, dc in far_first():
            send_to(1, places[dx, dl], chan_at[dz, dh, dc], tiles[dx, dl])

    for sig in range(2):

        def filter_step(number, carry):
            if sig == 0:

                frames_in(0, number).wait()
                frames_in(1, number).wait()

            filter_block(sig, number, lax.rem(number, 2), number - 1)
            return carry

        def transform_step(group, carry):
            transform(1, group)
            return carry

        if sig == 0:
            frames_in(0, 0).wait()
            frames_in(1, 0).wait()
            for chunk in range(2, BLOCKS):
                frames_in(0, chunk).start()
                frames_in(1, chunk).start()
            second_in.start()
            first_in.wait()
        filter_block(sig, 0, 0)
        lax.fori_loop(1, BLOCKS, filter_step, 0)
        for quad in range(SB // 4):
            first_stage(BLOCKS - 1, (BLOCKS - 1) % 2, quad)
        if sig == 0:
            pl.semaphore_wait(barrier, 66)
            for turn in range(1, 4):
                signal(ready.at[turn], chan, tile_at[8 - turn])
            second_in.wait()
            lax.fori_loop(0, 4, first_sends, 0)
        else:
            lax.fori_loop(0, 4, transform_step, 0)
            second_sends()
        got[sig * 256 + me] = msg[(sig * 4 + lax.rem(tile, 4)) * C2 + 2 * chan + lax.div(tile, 4)]

    to = lax.broadcasted_iota(jnp.int32, (256, 256), 0)
    come = lax.broadcasted_iota(jnp.int32, (256, 256), 1)
    sort = (to == (come % 8) * 32 + (come // 8 % 16) * 2 + come // 128).astype(jnp.bfloat16)

    others = pl.ds(0, 255)
    for sig in range(2):
        pltpu.make_async_copy(msg.at[others], got.at[others], recv.at[sig]).wait()
    for from_tile in range(8):
        right = jnp.concatenate(
            [
                jnp.concatenate(
                    [got[sig * 256 + from_tile * 32 + 16 * q : sig * 256 + from_tile * 32 + 16 * q + 16].reshape(128, LANES) for sig in range(2)], axis=0
                )
                for q in range(2)
            ],
            axis=1,
        )
        rows = jnp.dot(sort, right, preferred_element_type=jnp.float32)
        for q in range(2):
            here = slice(from_tile * 64 + 32 * q, from_tile * 64 + 32 * q + 32)
            part = rows[:, q * 128 : (q + 1) * 128]
            ordered[:, here, :] = part.astype(jnp.bfloat16).reshape(8, 32, LANES)
    everything = pl.ds(0, 510)
    pltpu.make_async_copy(msg.at[everything], got.at[everything], send).wait()


def correlate(x, out_hbm, out, osem):
    outs = [pltpu.make_async_copy(out.at[k], out_hbm.at[k], osem.at[k]) for k in range(8)]
    upper = lax.broadcasted_iota(jnp.int32, (256, 256), 0) <= lax.broadcasted_iota(jnp.int32, (256, 256), 1)
    for k in range(8):
        here = x[k]
        wide = here.astype(jnp.float32)
        turned = jnp.concatenate([wide[:, SPEC:], -wide[:, :SPEC]], axis=1).astype(jnp.bfloat16)

        def product(imag, lo, hi):
            left = (turned if imag else here)[lo * 256 : lo * 256 + 256]
            return lax.dot_general(left, here[hi * 256 : hi * 256 + 256], NT, preferred_element_type=jnp.float32)

        for lo in range(2):
            for hi in range(2):
                if lo != hi:
                    block = product(int(lo > hi), lo, hi)
                else:
                    block = jnp.where(upper, product(0, lo, hi), product(1, lo, hi))
                out[k, lo * 256 : lo * 256 + 256, hi * 256 : hi * 256 + 256] = block.astype(jnp.bfloat16)
        outs[k].start()
    for copy in outs:
        copy.wait()


def per_device(voltages, filter_taps):
    rows = NFFT // LANES
    frames = voltages.reshape(2, 2, FRAMES * rows, LANES).transpose(0, 2, 1, 3).reshape(2, FRAMES, 2 * rows, LANES)
    taps = filter_taps.reshape(2, 8, rows, LANES).transpose(0, 2, 1, 3).reshape(2 * rows * 8, LANES)
    tables = np.concatenate([second_table(), first_table()[None]], 0)
    hbm, vmem = pl.BlockSpec(memory_space=pl.ANY), pl.BlockSpec(memory_space=pltpu.VMEM)
    dma = pltpu.SemaphoreType.DMA
    ordered = pl.pallas_call(
        channelize,
        name="channelize",
        out_shape=jax.ShapeDtypeStruct((8, 512, LANES), jnp.bfloat16),
        in_specs=[hbm, vmem, hbm],
        out_specs=vmem,
        scratch_shapes=[
            pltpu.VMEM((2, FRAMES, 2 * rows, LANES), jnp.int32),
            pltpu.VMEM((3 * HALF, rows, LANES), jnp.float32),
            pltpu.VMEM(tables.shape[1:], jnp.bfloat16),
            pltpu.VMEM((R1,) + tables.shape[1:], jnp.bfloat16),
            pltpu.VMEM((2, SB, 2 * rows, LANES), jnp.bfloat16),
            pltpu.VMEM((SPEC * 64, LANES), jnp.float32),
            pltpu.VMEM((8 * C2, LANES), jnp.float32),
            pltpu.VMEM((512, 8, LANES), jnp.bfloat16),
            pltpu.VMEM((512, 8, LANES), jnp.bfloat16),
            dma((2, BLOCKS)),
            dma((2,)),
            dma,
            dma((2,)),
            pltpu.SemaphoreType.REGULAR((4,)),
        ],
        compiler_params=pltpu.CompilerParams(collective_id=0, has_side_effects=True, vmem_limit_bytes=52 << 20),
    )(frames, taps, jnp.asarray(tables))
    return pl.pallas_call(
        correlate,
        name="correlate",
        out_shape=jax.ShapeDtypeStruct((8, 512, 512), jnp.bfloat16),
        in_specs=[vmem],
        out_specs=hbm,
        scratch_shapes=[
            pltpu.VMEM((8, 512, 512), jnp.bfloat16),
            dma((8,)),
        ],
        compiler_params=pltpu.CompilerParams(vmem_limit_bytes=48 << 20),
    )(ordered)


def solution(mesh):
    return jax.shard_map(
        per_device,
        mesh=mesh,
        in_specs=(P(None, ("tile", "chan"), None), P()),
        out_specs=P(("chan", "tile"), None, None),
        check_vma=False,
    )
```

```python
import functools
import math

import jax
import jax.numpy as jnp
import ml_dtypes
import numpy as np
from jax import lax
from jax.experimental import pallas as pl
from jax.experimental.pallas import tpu as pltpu
from jax.sharding import PartitionSpec as P

MESH = pl.DeviceIdType.MESH
NFFT, TAPS, SPEC, KEEP = 4096, 16, 64, 2048
FRAMES = SPEC + TAPS - 1
LANES = 128
R1 = NFFT // LANES
C2 = KEEP // R1
SB = 16
BLOCKS = SPEC // SB
FIRST = SB + TAPS - 1
HALF = TAPS // 2
NT = (((1,), (1,)), ((), ()))


def split(values):
    high = values.astype(ml_dtypes.bfloat16)
    low = (values - high.astype(np.float64)).astype(ml_dtypes.bfloat16)
    return high, low


@functools.cache
def first_table():
    c1, j = np.meshgrid(np.arange(R1), np.arange(R1), indexing="ij")
    angle = 2 * math.pi * ((c1 * j) % R1) / R1
    cos, sin = np.cos(angle), np.sin(angle)
    unit = np.concatenate([np.concatenate([cos, sin], 1), np.concatenate([-sin, cos], 1)], 0)
    return np.concatenate(split(np.kron(np.eye(2), unit)), 1)


@functools.cache
def second_table():
    chan = np.arange(R1)[:, None, None] + R1 * np.arange(C2)[None, :, None]
    angle = 2 * math.pi * ((chan * np.arange(LANES)) % NFFT) / NFFT
    full = np.concatenate([np.cos(angle), -np.sin(angle)], 2) / (math.sqrt(NFFT) * math.sqrt(SPEC))
    return np.concatenate(split(full), 1)


Z_ORDER = (4, 3, 5, 2, 6, 1, 7, 0)


def chan_table():
    chan = lax.axis_index("chan")
    z, high, core = lax.div(chan, 4), lax.rem(lax.div(chan, 2), 2), lax.rem(chan, 2)
    z_part = [lax.rem(z + dz, 8) * 4 for dz in range(8)]
    y_part = [high * 2, 2 - high * 2]
    c_part = [core, 1 - core]
    return chan, {(dz, dh, dc): z_part[dz] + (y_part[dh] + c_part[dc]) for dz in range(8) for dh in range(2) for dc in range(2)}


def far_first():
    def hops(to):
        dz, dx, low, high, _ = to
        return min(dz, 8 - dz) + min(dx, 4 - dx) + (1 if low else 2 * high)

    every = [(dz, dx, low, high, dc) for dx in range(4) for low in range(2) for high in range(2) for dz in Z_ORDER for dc in range(2)]
    every = sorted((to for to in every if any(to)), key=lambda to: -hops(to))
    across, within = [to for to in every if to[0]], [to for to in every if not to[0]]
    order = []
    for i, to in enumerate(across):
        order.append(to)
        if i % 5 == 1 and within:
            order.append(within.pop(0))
    return order + within


def signal(sem, chan, tile):
    pl.semaphore_signal(sem, inc=1, device_id={"chan": chan, "tile": tile}, device_id_type=MESH)


def channelize(v_hbm, hraw, t_hbm, ordered, vbuf, hbuf, dbuf, wbuf, xs, af, sbuf, msg, got, vsem, csem, send, recv, ready):
    barrier = pltpu.get_barrier_semaphore()
    chan, chan_at = chan_table()
    tile = lax.axis_index("tile")
    tile_at = [lax.rem(tile + step, 8) for step in range(8)]
    me = tile * 32 + chan

    def frames_in(part, chunk):
        where = pl.ds(0, FIRST) if isinstance(chunk, int) and chunk == 0 else pl.ds(chunk * SB + TAPS - 1, SB)
        return pltpu.make_async_copy(v_hbm.at[part, where], vbuf.at[part, where], vsem.at[part, chunk])

    first_in = pltpu.make_async_copy(t_hbm.at[R1], dbuf, csem.at[0])
    second_in = pltpu.make_async_copy(t_hbm.at[pl.ds(0, R1)], wbuf, csem.at[1])
    frames_in(0, 0).start()
    frames_in(1, 0).start()
    first_in.start()
    frames_in(0, 1).start()
    frames_in(1, 1).start()

    for dz in Z_ORDER:
        for dx in range(2):
            for dh in range(2):
                for dc in range(2):
                    if dz or dx or dh or dc:
                        signal(barrier, chan_at[dz, dh, dc], tile_at[4 * dx])
    for turn in range(1, 4):
        signal(barrier, chan, tile_at[turn])

    for block in range(4):
        for i in range(HALF):
            even, odd = [
                hraw[pl.ds((tap // 8) * 256 + block * 64 + tap % 8, 8, stride=8), :] for tap in (2 * i, 2 * i + 1)
            ]
            rows = slice(block * 8, block * 8 + 8)
            hbuf[i, rows, :] = even
            hbuf[HALF + i, rows, :] = odd
            hbuf[2 * HALF + i, rows, :] = even + odd

    def filter_rows(sig, part, block, base):
        rows = slice(block * 8, block * 8 + 8)
        here = pl.ds(block * 16 + sig, 8, stride=2)
        window = vbuf[part, pl.ds(base, FIRST - 1), here, :].astype(jnp.float32).reshape(FIRST // 2, 2, 8, LANES)
        last = vbuf[part, pl.ds(base + FIRST - 1, 1), here, :].astype(jnp.float32)
        even, odd = window[:, 0], window[:, 1]
        ahead = jnp.concatenate([even[1:], last], axis=0)

        def short(which, values):
            total = hbuf[which * HALF, rows, :][None] * values[0 : SB // 2]
            for i in range(1, HALF):
                total = total + hbuf[which * HALF + i, rows, :][None] * values[i : i + SB // 2]
            return total

        shared = short(2, odd)
        first = short(0, even - odd) + shared
        second = short(1, ahead - odd) + shared
        return jnp.stack([first, second], axis=1).reshape(SB, 8, LANES)

    def first_stage(number, slot, quad):
        pairs = [xs[slot, quad * 4 + 2 * q : quad * 4 + 2 * q + 2].reshape(128, LANES) for q in range(2)]
        right = jnp.concatenate([jnp.concatenate([pair, pair], axis=0) for pair in pairs], axis=1)
        out = jnp.dot(dbuf[...], right, preferred_element_type=jnp.float32)
        for q in range(2):
            where = pl.ds(pl.multiple_of((number * SB + quad * 4 + 2 * q) * 64, 128), 128)
            af[where, :] = out[:, q * 128 : (q + 1) * 128]

    def filter_block(sig, number, slot, before=None, copies=()):
        base = number * SB
        for part in range(2):
            if copies:
                copies[part].wait()
            for pair in range(2):
                if before is not None:
                    first_stage(before, 1 - slot, part * 2 + pair)
                both = jnp.concatenate([filter_rows(sig, part, 2 * pair + i, base) for i in range(2)], axis=1)
                xs[slot, :, part * 32 + pair * 16 : part * 32 + pair * 16 + 16, :] = both.astype(jnp.bfloat16)

    def send_to(sig, place, to_chan, to_tile, slot):
        pltpu.make_async_remote_copy(
            src_ref=msg.at[place + 2 * to_chan],
            dst_ref=got.at[sig * 256 + me],
            send_sem=send,
            recv_sem=recv.at[slot],
            device_id={"chan": to_chan, "tile": to_tile},
            device_id_type=MESH,
        ).start()

    def transform(sig, group):
        for k in range(8):
            c1 = group * 8 + k
            real = af[pl.ds(c1, SPEC, stride=64), :]
            imag = af[pl.ds(R1 + c1, SPEC, stride=64), :]
            right = jnp.concatenate(
                [jnp.concatenate([real, -imag], axis=1), jnp.concatenate([imag, real], axis=1)], axis=0
            ).astype(jnp.bfloat16)
            out = lax.dot_general(wbuf[c1], right, NT, preferred_element_type=jnp.float32)
            sbuf[k * C2 : (k + 1) * C2, :] = out[:C2] + out[C2:]
        for c2 in range(C2):
            msg[(sig * 4 + group) * C2 + c2] = sbuf[pl.ds(c2, 8, stride=C2), :].astype(jnp.bfloat16)

    def first_sends(turn, carry):
        group = lax.rem(tile + turn, 4)
        transform(0, group)

        @pl.when(turn > 0)
        def _():
            pl.semaphore_wait(ready.at[turn], 1)

        own_half = lax.div(tile, 4)
        for dx in range(2):
            half = 1 - own_half if dx else own_half
            for dh in range(2):
                for dz in Z_ORDER:
                    for dc in range(2):
                        to = functools.partial(send_to, 0, group * C2 + half, chan_at[dz, dh, dc], half * 4 + group, 8)
                        if dx or dh or dz or dc:
                            to()
                        else:
                            pl.when(turn != 0)(to)
        return carry

    def second_sends():
        x, low = lax.div(tile, 2), lax.rem(tile, 2)
        x_at = [lax.rem(x + dx, 4) for dx in range(4)]
        low_at = [low, 1 - low]
        tiles = {(dx, dl): x_at[dx] * 2 + low_at[dl] for dx in range(4) for dl in range(2)}
        places = {to: (4 + lax.rem(at, 4)) * C2 + lax.div(at, 4) for to, at in tiles.items()}
        for dz, dx, dl, dh, dc in far_first():
            send_to(1, places[dx, dl], chan_at[dz, dh, dc], tiles[dx, dl], dx * 2 + dl)

    for sig in range(2):

        def filter_step(number, carry):
            if sig == 0:

                frames_in(0, number).wait()
                frames_in(1, number).wait()

            filter_block(sig, number, lax.rem(number, 2), number - 1)
            return carry

        def transform_step(group, carry):
            transform(1, group)
            return carry

        if sig == 0:
            filter_block(sig, 0, 0, copies=(frames_in(0, 0), frames_in(1, 0)))
            for chunk in range(2, BLOCKS):
                frames_in(0, chunk).start()
                frames_in(1, chunk).start()
            second_in.start()
            first_in.wait()
        else:
            filter_block(sig, 0, 0)
        lax.fori_loop(1, BLOCKS, filter_step, 0)
        for quad in range(SB // 4):
            first_stage(BLOCKS - 1, (BLOCKS - 1) % 2, quad)
        if sig == 0:
            pl.semaphore_wait(barrier, 66)
            for turn in range(1, 4):
                signal(ready.at[turn], chan, tile_at[8 - turn])
            second_in.wait()
            lax.fori_loop(0, 4, first_sends, 0)
        else:
            lax.fori_loop(0, 4, transform_step, 0)
            second_sends()
        got[sig * 256 + me] = msg[(sig * 4 + lax.rem(tile, 4)) * C2 + 2 * chan + lax.div(tile, 4)]

    to = lax.broadcasted_iota(jnp.int32, (256, 256), 0)
    come = lax.broadcasted_iota(jnp.int32, (256, 256), 1)
    sort = (to == (come % 8) * 32 + (come // 8 % 16) * 2 + come // 128).astype(jnp.bfloat16)

    others = pl.ds(0, 255)
    pltpu.make_async_copy(msg.at[others], got.at[others], recv.at[8]).wait()
    x, low = lax.div(tile, 2), lax.rem(tile, 2)
    for dx, dl in ((2, 1), (2, 0), (1, 1), (3, 1), (1, 0), (3, 0), (0, 1), (0, 0)):
        some = pl.ds(0, 32 if dx or dl else 31)
        pltpu.make_async_copy(msg.at[some], got.at[some], recv.at[dx * 2 + dl]).wait()
        from_tile = lax.rem(x + 4 - dx, 4) * 2 + (1 - low if dl else low)
        right = jnp.concatenate(
            [
                jnp.concatenate(
                    [got[pl.ds(sig * 256 + from_tile * 32 + 16 * q, 16)].reshape(128, LANES) for sig in range(2)], axis=0
                )
                for q in range(2)
            ],
            axis=1,
        )
        rows = jnp.dot(sort, right, preferred_element_type=jnp.float32)
        for q in range(2):
            here = pl.ds(pl.multiple_of(from_tile * 64 + 32 * q, 32), 32)
            part = rows[:, q * 128 : (q + 1) * 128]
            ordered[:, here, :] = part.astype(jnp.bfloat16).reshape(8, 32, LANES)
    everything = pl.ds(0, 510)
    pltpu.make_async_copy(msg.at[everything], got.at[everything], send).wait()


def correlate(x, out_hbm, out, osem):
    outs = [pltpu.make_async_copy(out.at[k], out_hbm.at[k], osem.at[k]) for k in range(8)]
    upper = lax.broadcasted_iota(jnp.int32, (256, 256), 0) <= lax.broadcasted_iota(jnp.int32, (256, 256), 1)
    for k in range(8):
        here = x[k]
        wide = here.astype(jnp.float32)
        turned = jnp.concatenate([wide[:, SPEC:], -wide[:, :SPEC]], axis=1).astype(jnp.bfloat16)

        def product(imag, lo, hi):
            left = (turned if imag else here)[lo * 256 : lo * 256 + 256]
            return lax.dot_general(left, here[hi * 256 : hi * 256 + 256], NT, preferred_element_type=jnp.float32)

        for lo in range(2):
            for hi in range(2):
                if lo != hi:
                    block = product(int(lo > hi), lo, hi)
                else:
                    block = jnp.where(upper, product(0, lo, hi), product(1, lo, hi))
                out[k, lo * 256 : lo * 256 + 256, hi * 256 : hi * 256 + 256] = block.astype(jnp.bfloat16)
        outs[k].start()
    for copy in outs:
        copy.wait()


def per_device(voltages, filter_taps):
    rows = NFFT // LANES
    frames = voltages.reshape(2, 2, FRAMES * rows, LANES).transpose(0, 2, 1, 3).reshape(2, FRAMES, 2 * rows, LANES)
    taps = filter_taps.reshape(2, 8, rows, LANES).transpose(0, 2, 1, 3).reshape(2 * rows * 8, LANES)
    tables = np.concatenate([second_table(), first_table()[None]], 0)
    hbm, vmem = pl.BlockSpec(memory_space=pl.ANY), pl.BlockSpec(memory_space=pltpu.VMEM)
    dma = pltpu.SemaphoreType.DMA
    ordered = pl.pallas_call(
        channelize,
        name="channelize",
        out_shape=jax.ShapeDtypeStruct((8, 512, LANES), jnp.bfloat16),
        in_specs=[hbm, vmem, hbm],
        out_specs=vmem,
        scratch_shapes=[
            pltpu.VMEM((2, FRAMES, 2 * rows, LANES), jnp.int32),
            pltpu.VMEM((3 * HALF, rows, LANES), jnp.float32),
            pltpu.VMEM(tables.shape[1:], jnp.bfloat16),
            pltpu.VMEM((R1,) + tables.shape[1:], jnp.bfloat16),
            pltpu.VMEM((2, SB, 2 * rows, LANES), jnp.bfloat16),
            pltpu.VMEM((SPEC * 64, LANES), jnp.float32),
            pltpu.VMEM((8 * C2, LANES), jnp.float32),
            pltpu.VMEM((512, 8, LANES), jnp.bfloat16),
            pltpu.VMEM((512, 8, LANES), jnp.bfloat16),
            dma((2, BLOCKS)),
            dma((2,)),
            dma,
            dma((9,)),
            pltpu.SemaphoreType.REGULAR((4,)),
        ],
        compiler_params=pltpu.CompilerParams(collective_id=0, has_side_effects=True, vmem_limit_bytes=52 << 20),
    )(frames, taps, jnp.asarray(tables))
    return pl.pallas_call(
        correlate,
        name="correlate",
        out_shape=jax.ShapeDtypeStruct((8, 512, 512), jnp.bfloat16),
        in_specs=[vmem],
        out_specs=hbm,
        scratch_shapes=[
            pltpu.VMEM((8, 512, 512), jnp.bfloat16),
            dma((8,)),
        ],
        compiler_params=pltpu.CompilerParams(vmem_limit_bytes=48 << 20),
    )(ordered)


def solution(mesh):
    return jax.shard_map(
        per_device,
        mesh=mesh,
        in_specs=(P(None, ("tile", "chan"), None), P()),
        out_specs=P(("chan", "tile"), None, None),
        check_vma=False,
    )
```

```python
import functools
import math

import jax
import jax.numpy as jnp
import ml_dtypes
import numpy as np
from jax import lax
from jax.experimental import pallas as pl
from jax.experimental.pallas import tpu as pltpu
from jax.sharding import PartitionSpec as P

MESH = pl.DeviceIdType.MESH
NFFT, TAPS, SPEC, KEEP = 4096, 16, 64, 2048
FRAMES = SPEC + TAPS - 1
LANES = 128
R1 = NFFT // LANES
C2 = KEEP // R1
SB = 16
BLOCKS = SPEC // SB
FIRST = SB + TAPS - 1
HALF = TAPS // 2
NT = (((1,), (1,)), ((), ()))


def split(values):
    high = values.astype(ml_dtypes.bfloat16)
    low = (values - high.astype(np.float64)).astype(ml_dtypes.bfloat16)
    return high, low


@functools.cache
def first_table():
    c1, j = np.meshgrid(np.arange(R1), np.arange(R1), indexing="ij")
    angle = 2 * math.pi * ((c1 * j) % R1) / R1
    cos, sin = np.cos(angle), np.sin(angle)
    unit = np.concatenate([np.concatenate([cos, sin], 1), np.concatenate([-sin, cos], 1)], 0)
    return np.concatenate(split(np.kron(np.eye(2), unit)), 1)


@functools.cache
def second_table():
    chan = np.arange(R1)[:, None, None] + R1 * np.arange(C2)[None, :, None]
    angle = 2 * math.pi * ((chan * np.arange(LANES)) % NFFT) / NFFT
    full = np.concatenate([np.cos(angle), -np.sin(angle)], 2) / (math.sqrt(NFFT) * math.sqrt(SPEC))
    return np.concatenate(split(full), 1)


Z_ORDER = (4, 3, 5, 2, 6, 1, 7, 0)


def chan_table():
    chan = lax.axis_index("chan")
    z, high, core = lax.div(chan, 4), lax.rem(lax.div(chan, 2), 2), lax.rem(chan, 2)
    z_part = [lax.rem(z + dz, 8) * 4 for dz in range(8)]
    y_part = [high * 2, 2 - high * 2]
    c_part = [core, 1 - core]
    return chan, {(dz, dh, dc): z_part[dz] + (y_part[dh] + c_part[dc]) for dz in range(8) for dh in range(2) for dc in range(2)}


def far_first():
    def hops(to):
        dz, dx, low, high, _ = to
        return min(dz, 8 - dz) + min(dx, 4 - dx) + (1 if low else 2 * high)

    every = [(dz, dx, low, high, dc) for dx in range(4) for low in range(2) for high in range(2) for dz in Z_ORDER for dc in range(2)]
    every = sorted((to for to in every if any(to)), key=lambda to: -hops(to))
    across, within = [to for to in every if to[0]], [to for to in every if not to[0]]
    order = []
    for i, to in enumerate(across):
        order.append(to)
        if i % 5 == 1 and within:
            order.append(within.pop(0))
    return order + within


def signal(sem, chan, tile):
    pl.semaphore_signal(sem, inc=1, device_id={"chan": chan, "tile": tile}, device_id_type=MESH)


def channelize(v_hbm, hraw, t_hbm, ordered, vbuf, hbuf, dbuf, wbuf, xs, af, sbuf, msg, got, vsem, csem, send, recv, ready):
    barrier = pltpu.get_barrier_semaphore()
    chan, chan_at = chan_table()
    tile = lax.axis_index("tile")
    tile_at = [lax.rem(tile + step, 8) for step in range(8)]
    me = tile * 32 + chan

    def frames_in(part, chunk):
        where = pl.ds(0, FIRST) if isinstance(chunk, int) and chunk == 0 else pl.ds(chunk * SB + TAPS - 1, SB)
        return pltpu.make_async_copy(v_hbm.at[part, where], vbuf.at[part, where], vsem.at[part, chunk])

    first_in = pltpu.make_async_copy(t_hbm.at[R1], dbuf, csem.at[0])
    second_in = pltpu.make_async_copy(t_hbm.at[pl.ds(0, R1)], wbuf, csem.at[1])
    frames_in(0, 0).start()
    frames_in(1, 0).start()
    first_in.start()
    frames_in(0, 1).start()
    frames_in(1, 1).start()

    for dz in Z_ORDER:
        for dx in range(2):
            for dh in range(2):
                for dc in range(2):
                    if dz or dx or dh or dc:
                        signal(barrier, chan_at[dz, dh, dc], tile_at[4 * dx])
    for turn in range(1, 4):
        signal(barrier, chan, tile_at[turn])

    for block in range(4):
        for i in range(HALF):
            even, odd = [
                hraw[pl.ds((tap // 8) * 256 + block * 64 + tap % 8, 8, stride=8), :] for tap in (2 * i, 2 * i + 1)
            ]
            rows = slice(block * 8, block * 8 + 8)
            hbuf[i, rows, :] = even
            hbuf[HALF + i, rows, :] = odd
            hbuf[2 * HALF + i, rows, :] = even + odd

    def filter_rows(sig, part, block, base):
        rows = slice(block * 8, block * 8 + 8)
        here = pl.ds(block * 16 + sig, 8, stride=2)
        window = vbuf[part, pl.ds(base, FIRST - 1), here, :].astype(jnp.float32).reshape(FIRST // 2, 2, 8, LANES)
        last = vbuf[part, pl.ds(base + FIRST - 1, 1), here, :].astype(jnp.float32)
        even, odd = window[:, 0], window[:, 1]
        ahead = jnp.concatenate([even[1:], last], axis=0)

        def short(which, values):
            total = hbuf[which * HALF, rows, :][None] * values[0 : SB // 2]
            for i in range(1, HALF):
                total = total + hbuf[which * HALF + i, rows, :][None] * values[i : i + SB // 2]
            return total

        shared = short(2, odd)
        first = short(0, even - odd) + shared
        second = short(1, ahead - odd) + shared
        return jnp.stack([first, second], axis=1).reshape(SB, 8, LANES)

    def first_stage(number, slot, quad):
        pairs = [xs[slot, quad * 4 + 2 * q : quad * 4 + 2 * q + 2].reshape(128, LANES) for q in range(2)]
        right = jnp.concatenate([jnp.concatenate([pair, pair], axis=0) for pair in pairs], axis=1)
        out = jnp.dot(dbuf[...], right, preferred_element_type=jnp.float32)
        for q in range(2):
            where = pl.ds(pl.multiple_of((number * SB + quad * 4 + 2 * q) * 64, 128), 128)
            af[where, :] = out[:, q * 128 : (q + 1) * 128]

    def filter_block(sig, number, slot, before=None):
        base = number * SB
        for part in range(2):
            for pair in range(2):
                if before is not None:
                    first_stage(before, 1 - slot, part * 2 + pair)
                both = jnp.concatenate([filter_rows(sig, part, 2 * pair + i, base) for i in range(2)], axis=1)
                xs[slot, :, part * 32 + pair * 16 : part * 32 + pair * 16 + 16, :] = both.astype(jnp.bfloat16)

    def send_to(sig, place, to_chan, to_tile, slot):
        pltpu.make_async_remote_copy(
            src_ref=msg.at[place + 2 * to_chan],
            dst_ref=got.at[sig * 256 + me],
            send_sem=send,
            recv_sem=recv.at[slot],
            device_id={"chan": to_chan, "tile": to_tile},
            device_id_type=MESH,
        ).start()

    def transform(sig, group):
        for k in range(8):
            c1 = group * 8 + k
            real = af[pl.ds(c1, SPEC, stride=64), :]
            imag = af[pl.ds(R1 + c1, SPEC, stride=64), :]
            right = jnp.concatenate(
                [jnp.concatenate([real, -imag], axis=1), jnp.concatenate([imag, real], axis=1)], axis=0
            ).astype(jnp.bfloat16)
            out = lax.dot_general(wbuf[c1], right, NT, preferred_element_type=jnp.float32)
            sbuf[k * C2 : (k + 1) * C2, :] = out[:C2] + out[C2:]
        for c2 in range(C2):
            msg[(sig * 4 + group) * C2 + c2] = sbuf[pl.ds(c2, 8, stride=C2), :].astype(jnp.bfloat16)

    def first_sends(turn, carry):
        group = lax.rem(tile + turn, 4)
        transform(0, group)

        @pl.when(turn > 0)
        def _():
            pl.semaphore_wait(ready.at[turn], 1)

        own_half = lax.div(tile, 4)
        for dx in range(2):
            half = 1 - own_half if dx else own_half
            for dh in range(2):
                for dz in Z_ORDER:
                    for dc in range(2):
                        to = functools.partial(send_to, 0, group * C2 + half, chan_at[dz, dh, dc], half * 4 + group, 8)
                        if dx or dh or dz or dc:
                            to()
                        else:
                            pl.when(turn != 0)(to)
        return carry

    def second_sends():
        x, low = lax.div(tile, 2), lax.rem(tile, 2)
        x_at = [lax.rem(x + dx, 4) for dx in range(4)]
        low_at = [low, 1 - low]
        tiles = {(dx, dl): x_at[dx] * 2 + low_at[dl] for dx in range(4) for dl in range(2)}
        places = {to: (4 + lax.rem(at, 4)) * C2 + lax.div(at, 4) for to, at in tiles.items()}
        for dz, dx, dl, dh, dc in far_first():
            send_to(1, places[dx, dl], chan_at[dz, dh, dc], tiles[dx, dl], dx * 2 + dl)

    for sig in range(2):

        def filter_step(number, carry):
            if sig == 0:

                frames_in(0, number).wait()
                frames_in(1, number).wait()

            filter_block(sig, number, lax.rem(number, 2), number - 1)
            return carry

        def transform_step(group, carry):
            transform(1, group)
            return carry

        if sig == 0:
            frames_in(0, 0).wait()
            frames_in(1, 0).wait()
            for chunk in range(2, BLOCKS):
                frames_in(0, chunk).start()
                frames_in(1, chunk).start()
            second_in.start()
            first_in.wait()
        filter_block(sig, 0, 0)
        lax.fori_loop(1, BLOCKS, filter_step, 0)
        for quad in range(SB // 4):
            first_stage(BLOCKS - 1, (BLOCKS - 1) % 2, quad)
        if sig == 0:
            pl.semaphore_wait(barrier, 66)
            for turn in range(1, 4):
                signal(ready.at[turn], chan, tile_at[8 - turn])
            second_in.wait()
            lax.fori_loop(0, 4, first_sends, 0)
        else:
            lax.fori_loop(0, 4, transform_step, 0)
            second_sends()
        got[sig * 256 + me] = msg[(sig * 4 + lax.rem(tile, 4)) * C2 + 2 * chan + lax.div(tile, 4)]

    to = lax.broadcasted_iota(jnp.int32, (256, 256), 0)
    come = lax.broadcasted_iota(jnp.int32, (256, 256), 1)
    sort = (to == (come % 8) * 32 + (come // 8 % 16) * 2 + come // 128).astype(jnp.bfloat16)

    others = pl.ds(0, 255)
    pltpu.make_async_copy(msg.at[others], got.at[others], recv.at[8]).wait()
    x, low = lax.div(tile, 2), lax.rem(tile, 2)
    for dx, dl in ((2, 1), (2, 0), (1, 1), (3, 1), (1, 0), (3, 0), (0, 1), (0, 0)):
        some = pl.ds(0, 32 if dx or dl else 31)
        pltpu.make_async_copy(msg.at[some], got.at[some], recv.at[dx * 2 + dl]).wait()
        from_tile = lax.rem(x + 4 - dx, 4) * 2 + (1 - low if dl else low)
        right = jnp.concatenate(
            [
                jnp.concatenate(
                    [got[pl.ds(sig * 256 + from_tile * 32 + 16 * q, 16)].reshape(128, LANES) for sig in range(2)], axis=0
                )
                for q in range(2)
            ],
            axis=1,
        )
        rows = jnp.dot(sort, right, preferred_element_type=jnp.float32)
        for q in range(2):
            here = pl.ds(pl.multiple_of(from_tile * 64 + 32 * q, 32), 32)
            part = rows[:, q * 128 : (q + 1) * 128]
            ordered[:, here, :] = part.astype(jnp.bfloat16).reshape(8, 32, LANES)
    everything = pl.ds(0, 510)
    pltpu.make_async_copy(msg.at[everything], got.at[everything], send).wait()


def correlate(x, out_hbm, out, osem):
    outs = [pltpu.make_async_copy(out.at[k], out_hbm.at[k], osem.at[k]) for k in range(8)]
    upper = lax.broadcasted_iota(jnp.int32, (256, 256), 0) <= lax.broadcasted_iota(jnp.int32, (256, 256), 1)
    for k in range(8):
        here = x[k]
        wide = here.astype(jnp.float32)
        turned = jnp.concatenate([wide[:, SPEC:], -wide[:, :SPEC]], axis=1).astype(jnp.bfloat16)

        def product(imag, lo, hi):
            left = (turned if imag else here)[lo * 256 : lo * 256 + 256]
            return lax.dot_general(left, here[hi * 256 : hi * 256 + 256], NT, preferred_element_type=jnp.float32)

        for lo in range(2):
            for hi in range(2):
                if lo != hi:
                    block = product(int(lo > hi), lo, hi)
                else:
                    block = jnp.where(upper, product(0, lo, hi), product(1, lo, hi))
                out[k, lo * 256 : lo * 256 + 256, hi * 256 : hi * 256 + 256] = block.astype(jnp.bfloat16)
        outs[k].start()
    for copy in outs:
        copy.wait()


def per_device(voltages, filter_taps):
    rows = NFFT // LANES
    frames = voltages.reshape(2, 2, FRAMES * rows, LANES).transpose(0, 2, 1, 3).reshape(2, FRAMES, 2 * rows, LANES)
    taps = filter_taps.reshape(2, 8, rows, LANES).transpose(0, 2, 1, 3).reshape(2 * rows * 8, LANES)
    tables = np.concatenate([second_table(), first_table()[None]], 0)
    hbm, vmem = pl.BlockSpec(memory_space=pl.ANY), pl.BlockSpec(memory_space=pltpu.VMEM)
    dma = pltpu.SemaphoreType.DMA
    ordered = pl.pallas_call(
        channelize,
        name="channelize",
        out_shape=jax.ShapeDtypeStruct((8, 512, LANES), jnp.bfloat16),
        in_specs=[hbm, vmem, hbm],
        out_specs=vmem,
        scratch_shapes=[
            pltpu.VMEM((2, FRAMES, 2 * rows, LANES), jnp.int32),
            pltpu.VMEM((3 * HALF, rows, LANES), jnp.float32),
            pltpu.VMEM(tables.shape[1:], jnp.bfloat16),
            pltpu.VMEM((R1,) + tables.shape[1:], jnp.bfloat16),
            pltpu.VMEM((2, SB, 2 * rows, LANES), jnp.bfloat16),
            pltpu.VMEM((SPEC * 64, LANES), jnp.float32),
            pltpu.VMEM((8 * C2, LANES), jnp.float32),
            pltpu.VMEM((512, 8, LANES), jnp.bfloat16),
            pltpu.VMEM((512, 8, LANES), jnp.bfloat16),
            dma((2, BLOCKS)),
            dma((2,)),
            dma,
            dma((9,)),
            pltpu.SemaphoreType.REGULAR((4,)),
        ],
        compiler_params=pltpu.CompilerParams(collective_id=0, has_side_effects=True, vmem_limit_bytes=52 << 20),
    )(frames, taps, jnp.asarray(tables))
    return pl.pallas_call(
        correlate,
        name="correlate",
        out_shape=jax.ShapeDtypeStruct((8, 512, 512), jnp.bfloat16),
        in_specs=[vmem],
        out_specs=hbm,
        scratch_shapes=[
            pltpu.VMEM((8, 512, 512), jnp.bfloat16),
            dma((8,)),
        ],
        compiler_params=pltpu.CompilerParams(vmem_limit_bytes=48 << 20),
    )(ordered)


def solution(mesh):
    return jax.shard_map(
        per_device,
        mesh=mesh,
        in_specs=(P(None, ("tile", "chan"), None), P()),
        out_specs=P(("chan", "tile"), None, None),
        check_vma=False,
    )
```

```python
import functools
import math

import jax
import jax.numpy as jnp
import ml_dtypes
import numpy as np
from jax import lax
from jax.experimental import pallas as pl
from jax.experimental.pallas import tpu as pltpu
from jax.sharding import PartitionSpec as P

MESH = pl.DeviceIdType.MESH
NFFT, TAPS, SPEC, KEEP = 4096, 16, 64, 2048
FRAMES = SPEC + TAPS - 1
LANES = 128
R1 = NFFT // LANES
C2 = KEEP // R1
SB = 16
BLOCKS = SPEC // SB
FIRST = SB + TAPS - 1
HALF = TAPS // 2
NT = (((1,), (1,)), ((), ()))


def split(values):
    high = values.astype(ml_dtypes.bfloat16)
    low = (values - high.astype(np.float64)).astype(ml_dtypes.bfloat16)
    return high, low


@functools.cache
def first_table():
    c1, j = np.meshgrid(np.arange(R1), np.arange(R1), indexing="ij")
    angle = 2 * math.pi * ((c1 * j) % R1) / R1
    cos, sin = np.cos(angle), np.sin(angle)
    unit = np.concatenate([np.concatenate([cos, sin], 1), np.concatenate([-sin, cos], 1)], 0)
    return np.concatenate(split(np.kron(np.eye(2), unit)), 1)


@functools.cache
def second_table():
    chan = np.arange(R1)[:, None, None] + R1 * np.arange(C2)[None, :, None]
    angle = 2 * math.pi * ((chan * np.arange(LANES)) % NFFT) / NFFT
    full = np.concatenate([np.cos(angle), -np.sin(angle)], 2) / (math.sqrt(NFFT) * math.sqrt(SPEC))
    return np.concatenate(split(full), 1)


Z_ORDER = (4, 3, 5, 2, 6, 1, 7, 0)


def chan_table():
    chan = lax.axis_index("chan")
    z, high, core = lax.div(chan, 4), lax.rem(lax.div(chan, 2), 2), lax.rem(chan, 2)
    z_part = [lax.rem(z + dz, 8) * 4 for dz in range(8)]
    y_part = [high * 2, 2 - high * 2]
    c_part = [core, 1 - core]
    return chan, {(dz, dh, dc): z_part[dz] + (y_part[dh] + c_part[dc]) for dz in range(8) for dh in range(2) for dc in range(2)}


def far_first():
    def hops(to):
        dz, dx, low, high, _ = to
        return min(dz, 8 - dz) + min(dx, 4 - dx) + (1 if low else 2 * high)

    every = [(dz, dx, low, high, dc) for dx in range(4) for low in range(2) for high in range(2) for dz in Z_ORDER for dc in range(2)]
    every = sorted((to for to in every if any(to)), key=lambda to: -hops(to))
    across, within = [to for to in every if to[0]], [to for to in every if not to[0]]
    order = []
    for i, to in enumerate(across):
        order.append(to)
        if i % 5 == 1 and within:
            order.append(within.pop(0))
    return order + within


def signal(sem, chan, tile):
    pl.semaphore_signal(sem, inc=1, device_id={"chan": chan, "tile": tile}, device_id_type=MESH)


def channelize(v_hbm, hraw, t_hbm, ordered, vbuf, hbuf, dbuf, wbuf, xs, af, sbuf, msg, got, vsem, csem, send, recv, ready):
    barrier = pltpu.get_barrier_semaphore()
    chan, chan_at = chan_table()
    tile = lax.axis_index("tile")
    tile_at = [lax.rem(tile + step, 8) for step in range(8)]
    me = tile * 32 + chan

    def frames_in(part, chunk):
        where = pl.ds(0, FIRST) if isinstance(chunk, int) and chunk == 0 else pl.ds(chunk * SB + TAPS - 1, SB)
        return pltpu.make_async_copy(v_hbm.at[part, where], vbuf.at[part, where], vsem.at[part, chunk])

    first_in = pltpu.make_async_copy(t_hbm.at[R1], dbuf, csem.at[0])

    def second_in(turn):
        where = pl.ds(lax.rem(tile + turn, 4) * 8, 8)
        return pltpu.make_async_copy(t_hbm.at[where], wbuf.at[where], csem.at[1 + turn])

    frames_in(0, 0).start()
    frames_in(1, 0).start()
    first_in.start()
    frames_in(0, 1).start()
    frames_in(1, 1).start()

    for dz in Z_ORDER:
        for dx in range(2):
            for dh in range(2):
                for dc in range(2):
                    if dz or dx or dh or dc:
                        signal(barrier, chan_at[dz, dh, dc], tile_at[4 * dx])
    for turn in range(1, 4):
        signal(barrier, chan, tile_at[turn])

    for block in range(4):
        for i in range(HALF):
            even, odd = [
                hraw[pl.ds((tap // 8) * 256 + block * 64 + tap % 8, 8, stride=8), :] for tap in (2 * i, 2 * i + 1)
            ]
            rows = slice(block * 8, block * 8 + 8)
            hbuf[i, rows, :] = even
            hbuf[HALF + i, rows, :] = odd
            hbuf[2 * HALF + i, rows, :] = even + odd

    def filter_rows(sig, part, block, base):
        rows = slice(block * 8, block * 8 + 8)
        here = pl.ds(block * 16 + sig, 8, stride=2)
        window = vbuf[part, pl.ds(base, FIRST - 1), here, :].astype(jnp.float32).reshape(FIRST // 2, 2, 8, LANES)
        last = vbuf[part, pl.ds(base + FIRST - 1, 1), here, :].astype(jnp.float32)
        even, odd = window[:, 0], window[:, 1]
        ahead = jnp.concatenate([even[1:], last], axis=0)

        def short(which, values):
            total = hbuf[which * HALF, rows, :][None] * values[0 : SB // 2]
            for i in range(1, HALF):
                total = total + hbuf[which * HALF + i, rows, :][None] * values[i : i + SB // 2]
            return total

        shared = short(2, odd)
        first = short(0, even - odd) + shared
        second = short(1, ahead - odd) + shared
        return jnp.stack([first, second], axis=1).reshape(SB, 8, LANES)

    def first_stage(number, slot, quad):
        pairs = [xs[slot, quad * 4 + 2 * q : quad * 4 + 2 * q + 2].reshape(128, LANES) for q in range(2)]
        right = jnp.concatenate([jnp.concatenate([pair, pair], axis=0) for pair in pairs], axis=1)
        out = jnp.dot(dbuf[...], right, preferred_element_type=jnp.float32)
        for q in range(2):
            where = pl.ds(pl.multiple_of((number * SB + quad * 4 + 2 * q) * 64, 128), 128)
            af[where, :] = out[:, q * 128 : (q + 1) * 128]

    def filter_block(sig, number, slot, before=None):
        base = number * SB
        for part in range(2):
            for pair in range(2):
                if before is not None:
                    first_stage(before, 1 - slot, part * 2 + pair)
                both = jnp.concatenate([filter_rows(sig, part, 2 * pair + i, base) for i in range(2)], axis=1)
                xs[slot, :, part * 32 + pair * 16 : part * 32 + pair * 16 + 16, :] = both.astype(jnp.bfloat16)

    def send_to(sig, place, to_chan, to_tile):
        pltpu.make_async_remote_copy(
            src_ref=msg.at[place + 2 * to_chan],
            dst_ref=got.at[sig * 256 + me],
            send_sem=send,
            recv_sem=recv.at[sig],
            device_id={"chan": to_chan, "tile": to_tile},
            device_id_type=MESH,
        ).start()

    def transform(sig, group):
        for k in range(8):
            c1 = group * 8 + k
            real = af[pl.ds(c1, SPEC, stride=64), :]
            imag = af[pl.ds(R1 + c1, SPEC, stride=64), :]
            right = jnp.concatenate(
                [jnp.concatenate([real, -imag], axis=1), jnp.concatenate([imag, real], axis=1)], axis=0
            ).astype(jnp.bfloat16)
            out = lax.dot_general(wbuf[c1], right, NT, preferred_element_type=jnp.float32)
            sbuf[k * C2 : (k + 1) * C2, :] = out[:C2] + out[C2:]
        for c2 in range(C2):
            msg[(sig * 4 + group) * C2 + c2] = sbuf[pl.ds(c2, 8, stride=C2), :].astype(jnp.bfloat16)

    def first_sends(turn, carry):
        group = lax.rem(tile + turn, 4)
        second_in(turn).wait()
        transform(0, group)

        @pl.when(turn > 0)
        def _():
            pl.semaphore_wait(ready.at[turn], 1)

        own_half = lax.div(tile, 4)
        for dx in range(2):
            half = 1 - own_half if dx else own_half
            for dh in range(2):
                for dz in Z_ORDER:
                    for dc in range(2):
                        to = functools.partial(send_to, 0, group * C2 + half, chan_at[dz, dh, dc], half * 4 + group)
                        if dx or dh or dz or dc:
                            to()
                        else:
                            pl.when(turn != 0)(to)
        return carry

    def second_sends():
        x, low = lax.div(tile, 2), lax.rem(tile, 2)
        x_at = [lax.rem(x + dx, 4) for dx in range(4)]
        low_at = [low, 1 - low]
        tiles = {(dx, dl): x_at[dx] * 2 + low_at[dl] for dx in range(4) for dl in range(2)}
        places = {to: (4 + lax.rem(at, 4)) * C2 + lax.div(at, 4) for to, at in tiles.items()}
        for dz, dx, dl, dh, dc in far_first():
            send_to(1, places[dx, dl], chan_at[dz, dh, dc], tiles[dx, dl])

    for sig in range(2):

        def filter_step(number, carry):
            if sig == 0:

                frames_in(0, number).wait()
                frames_in(1, number).wait()

            filter_block(sig, number, lax.rem(number, 2), number - 1)
            return carry

        def transform_step(group, carry):
            transform(1, group)
            return carry

        if sig == 0:
            frames_in(0, 0).wait()
            frames_in(1, 0).wait()
            for chunk in range(2, BLOCKS):
                frames_in(0, chunk).start()
                frames_in(1, chunk).start()
                if chunk == 2:
                    second_in(0).start()
            for turn in range(1, 4):
                second_in(turn).start()
            first_in.wait()
        filter_block(sig, 0, 0)
        lax.fori_loop(1, BLOCKS, filter_step, 0)
        for quad in range(SB // 4):
            first_stage(BLOCKS - 1, (BLOCKS - 1) % 2, quad)
        if sig == 0:
            pl.semaphore_wait(barrier, 66)
            for turn in range(1, 4):
                signal(ready.at[turn], chan, tile_at[8 - turn])
            lax.fori_loop(0, 4, first_sends, 0)
        else:
            lax.fori_loop(0, 4, transform_step, 0)
            second_sends()
        got[sig * 256 + me] = msg[(sig * 4 + lax.rem(tile, 4)) * C2 + 2 * chan + lax.div(tile, 4)]

    to = lax.broadcasted_iota(jnp.int32, (256, 256), 0)
    come = lax.broadcasted_iota(jnp.int32, (256, 256), 1)
    sort = (to == (come % 8) * 32 + (come // 8 % 16) * 2 + come // 128).astype(jnp.bfloat16)

    others = pl.ds(0, 255)
    for sig in range(2):
        pltpu.make_async_copy(msg.at[others], got.at[others], recv.at[sig]).wait()
    for from_tile in range(8):
        right = jnp.concatenate(
            [
                jnp.concatenate(
                    [got[sig * 256 + from_tile * 32 + 16 * q : sig * 256 + from_tile * 32 + 16 * q + 16].reshape(128, LANES) for sig in range(2)], axis=0
                )
                for q in range(2)
            ],
            axis=1,
        )
        rows = jnp.dot(sort, right, preferred_element_type=jnp.float32)
        for q in range(2):
            here = slice(from_tile * 64 + 32 * q, from_tile * 64 + 32 * q + 32)
            part = rows[:, q * 128 : (q + 1) * 128]
            ordered[:, here, :] = part.astype(jnp.bfloat16).reshape(8, 32, LANES)
    everything = pl.ds(0, 510)
    pltpu.make_async_copy(msg.at[everything], got.at[everything], send).wait()


def correlate(x, out_hbm, out, osem):
    outs = [pltpu.make_async_copy(out.at[k], out_hbm.at[k], osem.at[k]) for k in range(8)]
    upper = lax.broadcasted_iota(jnp.int32, (256, 256), 0) <= lax.broadcasted_iota(jnp.int32, (256, 256), 1)
    for k in range(8):
        here = x[k]
        wide = here.astype(jnp.float32)
        turned = jnp.concatenate([wide[:, SPEC:], -wide[:, :SPEC]], axis=1).astype(jnp.bfloat16)

        def product(imag, lo, hi):
            left = (turned if imag else here)[lo * 256 : lo * 256 + 256]
            return lax.dot_general(left, here[hi * 256 : hi * 256 + 256], NT, preferred_element_type=jnp.float32)

        for lo in range(2):
            for hi in range(2):
                if lo != hi:
                    block = product(int(lo > hi), lo, hi)
                else:
                    block = jnp.where(upper, product(0, lo, hi), product(1, lo, hi))
                out[k, lo * 256 : lo * 256 + 256, hi * 256 : hi * 256 + 256] = block.astype(jnp.bfloat16)
        outs[k].start()
    for copy in outs:
        copy.wait()


def per_device(voltages, filter_taps):
    rows = NFFT // LANES
    frames = voltages.reshape(2, 2, FRAMES * rows, LANES).transpose(0, 2, 1, 3).reshape(2, FRAMES, 2 * rows, LANES)
    taps = filter_taps.reshape(2, 8, rows, LANES).transpose(0, 2, 1, 3).reshape(2 * rows * 8, LANES)
    tables = np.concatenate([second_table(), first_table()[None]], 0)
    hbm, vmem = pl.BlockSpec(memory_space=pl.ANY), pl.BlockSpec(memory_space=pltpu.VMEM)
    dma = pltpu.SemaphoreType.DMA
    ordered = pl.pallas_call(
        channelize,
        name="channelize",
        out_shape=jax.ShapeDtypeStruct((8, 512, LANES), jnp.bfloat16),
        in_specs=[hbm, vmem, hbm],
        out_specs=vmem,
        scratch_shapes=[
            pltpu.VMEM((2, FRAMES, 2 * rows, LANES), jnp.int32),
            pltpu.VMEM((3 * HALF, rows, LANES), jnp.float32),
            pltpu.VMEM(tables.shape[1:], jnp.bfloat16),
            pltpu.VMEM((R1,) + tables.shape[1:], jnp.bfloat16),
            pltpu.VMEM((2, SB, 2 * rows, LANES), jnp.bfloat16),
            pltpu.VMEM((SPEC * 64, LANES), jnp.float32),
            pltpu.VMEM((8 * C2, LANES), jnp.float32),
            pltpu.VMEM((512, 8, LANES), jnp.bfloat16),
            pltpu.VMEM((512, 8, LANES), jnp.bfloat16),
            dma((2, BLOCKS)),
            dma((5,)),
            dma,
            dma((2,)),
            pltpu.SemaphoreType.REGULAR((4,)),
        ],
        compiler_params=pltpu.CompilerParams(collective_id=0, has_side_effects=True, vmem_limit_bytes=52 << 20),
    )(frames, taps, jnp.asarray(tables))
    return pl.pallas_call(
        correlate,
        name="correlate",
        out_shape=jax.ShapeDtypeStruct((8, 512, 512), jnp.bfloat16),
        in_specs=[vmem],
        out_specs=hbm,
        scratch_shapes=[
            pltpu.VMEM((8, 512, 512), jnp.bfloat16),
            dma((8,)),
        ],
        compiler_params=pltpu.CompilerParams(vmem_limit_bytes=48 << 20),
    )(ordered)


def solution(mesh):
    return jax.shard_map(
        per_device,
        mesh=mesh,
        in_specs=(P(None, ("tile", "chan"), None), P()),
        out_specs=P(("chan", "tile"), None, None),
        check_vma=False,
    )
```
